128 devices in a mesh: leaf: 8 (over z, core), seq: 16 (over y, x).
Axes of the slice: x: 4, y: 4, z: 4, core: 2. Of those that a mesh axis runs over, the one named last changes fastest.
Arguments:
- hidden_in: bfloat16 [32768, 5120], P(('leaf', 'seq')), parts along dimension 0, may hold values from -6 to 6
- queries: bfloat16 [32768, 1024], P(('leaf', 'seq')), parts along dimension 0, may hold values from -32 to 32
- keys: bfloat16 [32768, 128], P(('leaf', 'seq')), parts along dimension 0, may hold values from -4 to 4
- values: bfloat16 [32768, 128], P(('leaf', 'seq')), parts along dimension 0, may hold values from -6 to 6
- out_grad: bfloat16 [32768, 1024], P(('leaf', 'seq')), parts along dimension 0, may hold values from -6 to 6
- parents: int32 [256], P('leaf'), parts along dimension 0, may hold values from -1 to 30, as said below
Outputs:
- query_grad: bfloat16 [32768, 1024], P(('leaf', 'seq')), parts along dimension 0
- proj_grad: float32 [40960, 256], P(('leaf', 'seq')), parts along dimension 0
The draws below stay inside these ranges and needn't reach their ends.
There are 8 independent parts, one for each index of `leaf`. The reference program is written for one: setup_inputs(seed, part) draws one part's arguments, and reference() takes and returns one part's arrays. A program takes and returns all parts, laid end to end along the dimension named above; each array names one. Nothing has to cross between parts.
Inputs may be any that keep to these rules, and one draw needn't show every extreme that they name: Segments are in depth-first order: a parent is an earlier segment. Following parents from any segment passes at most 16 segments before a root, and exactly 16 for some segment.
All inputs are finite; a program needn't handle non-finite values.
Results may differ from the reference program's by a relative error of at most 0.006.
Values may be sent and summed in bfloat16 or wider, within the bound.
A program may use at most 128 MiB of HBM per device.

```python
import jax
import jax.numpy as jnp
from jax import lax

D = 5120
GROUP = 8
HD = 128
SEG = 128
TOKENS = 4096
NSEG = 32
DEPTH = 16


def draw_keys(key, part):
    key = jax.random.fold_in(key, 1)
    base = jnp.clip(jax.random.normal(key, (TOKENS, HD)), -4.0, 4.0)
    return base.astype(jnp.bfloat16)


def draw_queries(key, part):
    key = jax.random.fold_in(key, 2)
    base = jnp.clip(jax.random.normal(key, (TOKENS, GROUP, HD)), -4.0, 4.0)
    return base.reshape(TOKENS, GROUP * HD).astype(jnp.bfloat16)


def draw_parents(key, part):
    key = jax.random.fold_in(key, 3)
    grow_key, jump_key, start_key = jax.random.split(key, 3)
    grow_draw = jax.random.randint(grow_key, (NSEG,), 0, 4)
    jump_draw = jax.random.randint(jump_key, (NSEG,), 0, 1 << 20)
    chain_start = jax.random.randint(start_key, (), 0, NSEG - DEPTH)

    def step(previous, index):
        deeper = previous + 1
        other = jump_draw[index] % (previous + 1)
        depth = jnp.where((grow_draw[index] != 0) & (deeper <= DEPTH), deeper, other)
        depth = jnp.where(index == 0, 0, depth)
        depth = jnp.where((index >= chain_start) & (index <= chain_start + DEPTH), index - chain_start, depth)
        return (depth, depth)
    indices = jnp.arange(NSEG, dtype=jnp.int32)
    final_depth, depths = lax.scan(step, jnp.int32(0), indices)
    candidate = (depths[None, :] == depths[:, None] - 1) & (indices[None, :] < indices[:, None])
    parent_of = jnp.max(jnp.where(candidate, indices[None, :], -1), axis=1)
    return jnp.where(depths == 0, -1, parent_of).astype(jnp.int32)


def block_levels(stream_key, shape, shards, smallest, largest):
    def one(position, shards_of):
        heights = jax.random.uniform(jax.random.fold_in(jax.random.fold_in(stream_key, 6), position), (shards_of,), jnp.float32, smallest / len(shards), largest / len(shards))
        return jnp.repeat(jnp.exp(heights), shape[position] // shards_of).reshape((-1,) + (1,) * (len(shape) - position - 1))

    factor_of = one(*shards[0])
    for cut in shards[1:]:
        factor_of = factor_of * one(*cut)
    return factor_of


def scatter_about(key, extent, scale, bound, shards=(), kind=jnp.bfloat16):
    values = scale * jax.random.normal(key, extent, jnp.float32)
    if shards:
        values = values * block_levels(key, extent, shards, -0.22, 0.18)
    return jnp.clip(values, -bound, bound).astype(kind)


def setup_inputs(seed: int = 0, part: int = 0) -> dict:
    seeds = jax.random.split(jax.random.key(seed), 7)
    own_keys = jax.random.split(jax.random.fold_in(seeds[6], part), 7)
    hidden_in = scatter_about(own_keys[0], (TOKENS, D), 1.0, 6.0, ((0, 16),))
    queries = draw_queries(jax.random.fold_in(jax.random.fold_in(seeds[6], part), 71), part)
    keys = draw_keys(jax.random.fold_in(jax.random.fold_in(seeds[6], part), 71), part)
    values = scatter_about(own_keys[3], (TOKENS, HD), 1.0, 6.0, ((0, 16),))
    out_grad = scatter_about(own_keys[4], (TOKENS, GROUP * HD), 1.0, 6.0, ((0, 16),))
    parents = draw_parents(jax.random.fold_in(jax.random.fold_in(seeds[6], part), 71), part)
    return {"hidden_in": hidden_in, "queries": queries, "keys": keys, "values": values, "out_grad": out_grad, "parents": parents}


def ancestry(parents):
    count = parents.shape[0]
    indices = jnp.arange(count, dtype=jnp.int32)
    reach = (parents[:, None] == indices[None, :]).astype(jnp.float32)
    for doubling in range(count.bit_length()):
        reach = jnp.minimum(reach + jnp.dot(reach, reach, precision=lax.Precision.HIGHEST), 1.0)
    return reach > 0.5


def pair_mask(ancestors, query_start, query_count, key_start, key_count, seg_len):
    query_first = jnp.asarray(query_start).astype(jnp.int32)
    key_first = jnp.asarray(key_start).astype(jnp.int32)
    query_segs = query_count // seg_len
    key_segs = key_count // seg_len
    coarse = lax.dynamic_slice(ancestors, ((query_first // seg_len).astype(jnp.int32), (key_first // seg_len).astype(jnp.int32)), (query_segs, key_segs))
    coarse = jnp.broadcast_to(coarse[:, None, :, None], (query_segs, seg_len, key_segs, seg_len)).reshape(query_count, key_count)
    query_pos = query_first + jnp.arange(query_count, dtype=jnp.int32)
    key_pos = key_first + jnp.arange(key_count, dtype=jnp.int32)
    same_seg = (query_pos[:, None] // seg_len) == (key_pos[None, :] // seg_len)
    return coarse | (same_seg & (key_pos[None, :] <= query_pos[:, None]))


def reference(hidden_in, queries, keys, values, out_grad, parents):
    ancestors = ancestry(parents)
    scale = HD ** -0.5
    block_len = min(TOKENS, 512)
    block_count = TOKENS // block_len
    key_wide = keys.astype(jnp.float32)
    value_wide = values.astype(jnp.float32)

    def step(carry, index):
        key_acc, value_acc = carry
        start = (index * block_len).astype(jnp.int32)
        block_queries = lax.dynamic_slice_in_dim(queries, start, block_len, 0).reshape(block_len, GROUP, HD).astype(jnp.float32)
        block_grads = lax.dynamic_slice_in_dim(out_grad, start, block_len, 0).reshape(block_len, GROUP, HD).astype(jnp.float32)
        mask = pair_mask(ancestors, start, block_len, 0, TOKENS, SEG)
        scores = jnp.einsum("qgd,kd->gqk", block_queries, key_wide) * scale
        scores = jnp.where(mask[None], scores, -jnp.inf)
        top = jnp.max(scores, axis=-1, keepdims=True)
        log_total = top + jnp.log(jnp.sum(jnp.exp(scores - top), axis=-1, keepdims=True))
        probs = jnp.exp(scores - log_total)
        probs_low = lax.optimization_barrier(probs.astype(jnp.bfloat16)).astype(jnp.float32)
        attended = jnp.einsum("gqk,kd->qgd", probs_low, value_wide)
        delta = jnp.sum(block_grads * attended, axis=-1).T[..., None]
        dprobs = jnp.einsum("qgd,kd->gqk", block_grads, value_wide)
        dscores = lax.optimization_barrier((probs * (dprobs - delta)).astype(jnp.bfloat16)).astype(jnp.float32)
        query_part = (jnp.einsum("gqk,kd->qgd", dscores, key_wide) * scale).reshape(block_len, GROUP * HD).astype(jnp.bfloat16)
        key_acc = key_acc + jnp.einsum("gqk,qgd->kd", dscores, block_queries)
        value_acc = value_acc + jnp.einsum("gqk,qgd->kd", probs_low, block_grads)
        return (key_acc, value_acc), query_part

    init = (jnp.zeros((TOKENS, HD), jnp.float32), jnp.zeros((TOKENS, HD), jnp.float32))
    (key_acc, value_acc), parts_out = lax.scan(step, init, jnp.arange(block_count, dtype=jnp.int32))
    query_grad = parts_out.reshape(TOKENS, GROUP * HD)
    key_value_grad = jnp.concatenate([key_acc * scale, value_acc], axis=-1).astype(jnp.bfloat16)
    proj_grad = lax.dot_general(hidden_in, key_value_grad, (((0,), (0,)), ((), ())), preferred_element_type=jnp.float32)
    return query_grad, proj_grad
```

```python
import functools

import jax
import jax.numpy as jnp
from jax import lax
from jax.experimental import pallas as pl
from jax.experimental.pallas import tpu as pltpu
from jax.sharding import PartitionSpec as P

BF, F32 = jnp.bfloat16, jnp.float32
MESH = pl.DeviceIdType.MESH
SIDE = 4
RANKS = SIDE * SIDE
SEG, HD, GROUP = 128, 128, 8
SEGS = 2 * RANKS
DEPTH = 16
SLOTS = DEPTH + 1
KEYS = SLOTS * SEG
PAIRS = GROUP // 2
UNITS = 2 * PAIRS
W = 2 * SEG
MC = 544
D = 5120
DCOLS = D // RANKS
LOG2E = 1.4426950408889634
SCALE = HD ** -0.5
PEN = 1e30
STEPS = (1, 3, 2)


def dot(a, b):
    return jnp.dot(a, b, preferred_element_type=F32)


def place():
    me = lax.axis_index("seq")
    return me, me // SIDE, lax.rem(me, SIDE)


def at(dy, dx):
    _, y, x = place()
    return lax.rem(y + dy + SIDE, SIDE) * SIDE + lax.rem(x + dx + SIDE, SIDE)


def remote(src, dst, send, recv, rank):
    return pltpu.make_async_remote_copy(
        src, dst, send, recv, device_id={"seq": rank}, device_id_type=MESH
    )


def loop(count, body):
    def step(index, carry):
        body(index)
        return carry

    lax.fori_loop(0, count, step, 0)


def score_unit(u, kc, qt, e, mxs):
    t = u // PAIRS
    weights = qt[u]
    key = lax.broadcasted_iota(jnp.int32, (SEG, W), 0)
    row = lax.broadcasted_iota(jnp.int32, (SEG, W), 1)
    row = jnp.where(row >= SEG, row - SEG, row)
    mx = jnp.full((8, W), -3e38, F32)
    for start in range(0, KEYS, MC):
        s = dot(kc[t, pl.ds(start, MC), :], weights)
        if start + MC == KEYS:
            own = jnp.where(key <= row, s[MC - SEG :], -PEN)
            s = jnp.concatenate([s[: MC - SEG], own], axis=0)
        e[u, pl.ds(start, MC), :] = s
        mx = jnp.maximum(mx, jnp.max(s.reshape(MC // 8, 8, W), axis=0))
    mxs[u] = mx


def prob_unit(u, slots, e, mxs, inv, p):
    t = u // PAIRS
    m = jnp.max(mxs[u], axis=0, keepdims=True) * (SCALE * LOG2E)
    acc = jnp.zeros((8, W), F32)
    for i in range(SLOTS):
        rows = pl.ds(i * SEG, SEG)
        shift = m
        if i < DEPTH:
            shift = m + jnp.where(slots[t, i] == SEGS, jnp.float32(PEN), jnp.float32(0.0))
        x = jnp.exp2(e[u, rows, :] * (SCALE * LOG2E) - shift)
        e[u, rows, :] = x
        acc = acc + jnp.sum(x.reshape(SEG // 8, 8, W), axis=0)
    r = 1.0 / jnp.sum(acc, axis=0, keepdims=True)
    inv[u] = jnp.broadcast_to(r, (8, W))
    for i in range(SLOTS):
        rows = pl.ds(i * SEG, SEG)
        p[u, rows, :] = (e[u, rows, :] * r).astype(BF)


def delta_unit(u, vct, gt, p, delta):
    o = dot(vct[u // PAIRS], p[u])
    d = jnp.sum(gt[u].astype(F32) * o, axis=0, keepdims=True)
    delta[u] = jnp.broadcast_to(d, (8, W))


def side_grad(t, lhs, rhs, acc):
    total = dot(lhs[t * PAIRS], rhs[t * PAIRS])
    for h in range(1, PAIRS):
        total += dot(lhs[t * PAIRS + h], rhs[t * PAIRS + h])
    acc[t, pl.ds(0, SLOTS)] = total.reshape(SLOTS, SEG, HD)
    acc[t, SLOTS] = jnp.zeros((SEG, HD), F32)


def ds_unit(u, vc, gt, e, inv, delta, ds):
    t = u // PAIRS
    weights = gt[u]
    r = inv[u, 0:1, :]
    d = delta[u, 0:1, :]
    for start in range(0, KEYS, MC):
        rows = pl.ds(start, MC)
        dp = dot(vc[t, rows, :], weights)
        ds[u, rows, :] = (e[u, rows, :] * r * (dp - d)).astype(BF)


def dq_unit(u, kct, ds, dq):
    t = u // PAIRS
    g = (dot(kct[t], ds[u]) * SCALE).T.astype(BF)
    first = lax.rem(u, PAIRS) * W
    rows = pl.ds(pl.multiple_of(t * SEG, SEG), SEG)
    for k in range(2):
        dq[rows, pl.ds(pl.multiple_of(first + k * HD, HD), HD)] = g[k * SEG : (k + 1) * SEG]


class Gather:
    def __init__(self, buf, send, recv):
        self.buf, self.send, self.recv = buf, send, recv
        self.copies = {}

    def shift(self, half, first, second):
        return at(second, first) if half == 0 else at(first, second)

    def start(self, half, p, q, to_p, to_q):
        origin = 2 * self.shift(half, -p, -q) + half
        target = self.shift(half, to_p - p, to_q - q)
        sem = (half, to_p * SIDE + to_q)
        copy = remote(
            self.buf.at[origin], self.buf.at[origin], self.send.at[sem], self.recv.at[sem], target
        )
        copy.start()
        self.copies[half, to_p, to_q] = copy

    def own(self):
        for step in STEPS:
            for half in range(2):
                self.start(half, 0, 0, step, 0)
        for step in STEPS:
            for half in range(2):
                self.start(half, 0, 0, 0, step)

    def forward(self):
        for p in STEPS:
            for half in range(2):
                self.copies[half, p, 0].wait_recv()
                for q in STEPS:
                    self.start(half, p, 0, p, q)

    def arrive(self):
        for (half, p, q), copy in self.copies.items():
            if q:
                copy.wait_recv()

    def drain(self):
        for copy in self.copies.values():
            copy.wait_send()


class Reduce:
    def __init__(self, stage, got, mid, last, send, recv):
        self.stage, self.got, self.mid, self.last = stage, got, mid, last
        self.send, self.recv = send, recv
        self.first, self.second = {}, {}

    def put(self, dest, low, high):
        y, x = dest // SIDE, lax.rem(dest, SIDE)
        self.stage[0, x, y] = low.astype(BF)
        self.stage[1, y, x] = high.astype(BF)

    def start(self):
        _, y, x = place()
        for step in STEPS:
            for half in range(2):
                column = lax.rem((x, y)[half] + step, SIDE)
                target = (at(0, step), at(step, 0))[half]
                self.first[half, step] = remote(
                    self.stage.at[half, column],
                    self.got.at[half, step - 1],
                    self.send.at[half, 0, step],
                    self.recv.at[half, 0, step],
                    target,
                )
                self.first[half, step].start()

    def middle(self):
        _, y, x = place()
        for half in range(2):
            for step in STEPS:
                self.first[half, step].wait_recv()
            here = (x, y)[half]
            for k in range(SIDE):
                total = self.stage[half, here, k].astype(F32)
                for step in STEPS:
                    total += self.got[half, step - 1, k].astype(F32)
                self.mid[half, k] = total.astype(BF)
            for step in STEPS:
                row = lax.rem((y, x)[half] + step, SIDE)
                target = (at(step, 0), at(0, step))[half]
                self.second[half, step] = remote(
                    self.mid.at[half, row],
                    self.last.at[half, step - 1],
                    self.send.at[half, 1, step],
                    self.recv.at[half, 1, step],
                    target,
                )
                self.second[half, step].start()

    def finish(self):
        _, y, x = place()
        totals = []
        for half in range(2):
            for step in STEPS:
                self.second[half, step].wait_recv()
            total = self.mid[half, (y, x)[half]].astype(F32)
            for step in STEPS:
                total += self.last[half, step - 1].astype(F32)
            totals.append(total)
        return totals

    def drain(self):
        for copy in [*self.first.values(), *self.second.values()]:
            copy.wait_send()


def table_kernel(parents, slots, where_to):
    me, _, _ = place()
    for t in range(2):
        cur = parents[2 * me + t]
        for i in range(DEPTH):
            slots[t, i] = jnp.where(cur >= 0, cur, SEGS)
            cur = jnp.where(cur >= 0, parents[jnp.maximum(cur, 0)], -1)

    def find(j):
        for t in range(2):
            found = jnp.where(j == 2 * me + t, DEPTH, SLOTS)
            for i in range(DEPTH):
                found = jnp.where(slots[t, i] == j, i, found)
            where_to[t, j] = found

    loop(SEGS, find)


def kernel(
    hid_ref, q_ref, k_ref, v_ref, g_ref, slots, where_to,
    dq_ref, proj_ref,
    hid, hid_t, q, g, k_all, v_all, kc, vc, kct, vct, qt, gt, qs, gs,
    e, p, mxs, inv, delta, dva, dka, low,
    kv_stage, kv_got, kv_mid, kv_last, pr_stage, pr_got, pr_mid, pr_last,
    local_sem, gather_send, gather_recv, sum_send, sum_recv,
):
    me, y, x = place()
    locals_ = [
        pltpu.make_async_copy(src, dst, local_sem.at[i])
        for i, (src, dst) in enumerate(((q_ref, q), (g_ref, g), (hid_ref, hid)))
    ]
    for copy in locals_:
        copy.start()

    barrier = pltpu.get_barrier_semaphore()
    for step in STEPS:
        for mate in (at(0, step), at(step, 0)):
            pl.semaphore_signal(barrier, inc=1, device_id={"seq": mate}, device_id_type=MESH)
    for half in range(2):
        k_all[2 * me + half] = k_ref[half * SEG : (half + 1) * SEG, :]
        v_all[2 * me + half] = v_ref[half * SEG : (half + 1) * SEG, :]
    pl.semaphore_wait(barrier, 6)

    keys = Gather(k_all, gather_send.at[0], gather_recv.at[0])
    vals = Gather(v_all, gather_send.at[1], gather_recv.at[1])
    keys.own()
    vals.own()

    locals_[0].wait()
    locals_[1].wait()

    def prepare(u):
        t = u // PAIRS
        first = lax.rem(u, PAIRS) * W
        rows = pl.ds(pl.multiple_of(t * SEG, SEG), SEG)
        for src, turned, stacked in ((q, qt, qs), (g, gt, gs)):
            for k in range(2):
                block = src[rows, pl.ds(pl.multiple_of(first + k * HD, HD), HD)]
                stacked[u, pl.ds(k * SEG, SEG), :] = block
                turned[u, :, pl.ds(k * SEG, SEG)] = block.T

    loop(UNITS, prepare)
    keys.forward()
    vals.forward()

    locals_[2].wait()

    def turn(c):
        cols = pl.ds(pl.multiple_of(c * HD, HD), HD)
        hid_t[cols, :] = hid[:, cols].T

    loop(D // HD, turn)

    def collect(source, rows_out, cols_out):
        for t in range(2):
            if source is k_all:
                head = source[2 * me + t, 0:16, :].astype(F32)[0:1]
                source[SEGS] = jnp.broadcast_to(head, (SEG, HD)).astype(BF)
            for i in range(SLOTS):
                block = source[slots[t, i]] if i < DEPTH else source[2 * me + t]
                rows_out[t, pl.ds(i * SEG, SEG), :] = block
                cols_out[t, :, pl.ds(i * SEG, SEG)] = block.T

    keys.arrive()
    collect(k_all, kc, kct)
    loop(UNITS, lambda u: score_unit(u, kc, qt, e, mxs))
    loop(UNITS, lambda u: prob_unit(u, slots, e, mxs, inv, p))

    vals.arrive()
    v_all[SEGS] = jnp.zeros((SEG, HD), BF)
    collect(v_all, vc, vct)
    loop(UNITS, lambda u: delta_unit(u, vct, gt, p, delta))

    def spread(acc, reduce):
        def put(dest):
            blocks = []
            for half in range(2):
                block = jnp.zeros((SEG, HD), F32)
                for t in range(2):
                    block += acc[t, where_to[t, 2 * dest + half]]
                blocks.append(block)
            reduce.put(dest, *blocks)

        loop(RANKS, put)
        reduce.start()

    def make(i, stage, got, mid, last):
        j = i % 2
        return Reduce(
            stage.at[j], got.at[j], mid.at[j], last.at[j], sum_send.at[i], sum_recv.at[i]
        )

    dv = make(0, kv_stage, kv_got, kv_mid, kv_last)
    dk = make(1, kv_stage, kv_got, kv_mid, kv_last)
    pv = make(2, pr_stage, pr_got, pr_mid, pr_last)
    pk = make(3, pr_stage, pr_got, pr_mid, pr_last)

    def project(reduce, grad, scale):
        for half, total in enumerate(grad.finish()):
            low[pl.ds(half * SEG, SEG), :] = (total * scale).astype(BF)
        weights = low[...]

        def put(dest):
            rows = pl.ds(pl.multiple_of(dest * DCOLS, 64), DCOLS)
            out = dot(hid_t[rows, :], weights)
            reduce.put(dest, out[: DCOLS // 2], out[DCOLS // 2 :])

        loop(RANKS, put)
        reduce.start()

    for t in range(2):
        side_grad(t, p, gs, dva)
    spread(dva, dv)
    loop(UNITS, lambda u: ds_unit(u, vc, gt, e, inv, delta, p))
    dv.middle()
    for t in range(2):
        side_grad(t, p, qs, dka)
    spread(dka, dk)
    project(pv, dv, 1.0)
    loop(UNITS, lambda u: dq_unit(u, kct, p, dq_ref))
    dk.middle()
    pv.middle()
    project(pk, dk, SCALE)
    pk.middle()
    for half, total in enumerate(pv.finish()):
        proj_ref[pl.ds(half * (DCOLS // 2), DCOLS // 2), pl.ds(HD, HD)] = total
    for half, total in enumerate(pk.finish()):
        proj_ref[pl.ds(half * (DCOLS // 2), DCOLS // 2), pl.ds(0, HD)] = total
    for part in (keys, vals, dv, dk, pv, pk):
        part.drain()


def on_device(hidden_in, queries, keys, values, out_grad, parents):
    vmem = pl.BlockSpec(memory_space=pltpu.VMEM)
    hbm = pl.BlockSpec(memory_space=pl.ANY)
    smem = pl.BlockSpec(memory_space=pltpu.SMEM)
    tokens = 2 * SEG
    half = DCOLS // 2
    scratch = [
        pltpu.VMEM((tokens, D), BF),
        pltpu.VMEM((D, tokens), BF),
        pltpu.VMEM((tokens, GROUP * HD), BF),
        pltpu.VMEM((tokens, GROUP * HD), BF),
        pltpu.VMEM((SEGS + 1, SEG, HD), BF),
        pltpu.VMEM((SEGS + 1, SEG, HD), BF),
        pltpu.VMEM((2, KEYS, HD), BF),
        pltpu.VMEM((2, KEYS, HD), BF),
        pltpu.VMEM((2, HD, KEYS), BF),
        pltpu.VMEM((2, HD, KEYS), BF),
        pltpu.VMEM((UNITS, HD, W), BF),
        pltpu.VMEM((UNITS, HD, W), BF),
        pltpu.VMEM((UNITS, W, HD), BF),
        pltpu.VMEM((UNITS, W, HD), BF),
        pltpu.VMEM((UNITS, KEYS, W), F32),
        pltpu.VMEM((UNITS, KEYS, W), BF),
        pltpu.VMEM((UNITS, 8, W), F32),
        pltpu.VMEM((UNITS, 8, W), F32),
        pltpu.VMEM((UNITS, 8, W), F32),
        pltpu.VMEM((2, SLOTS + 1, SEG, HD), F32),
        pltpu.VMEM((2, SLOTS + 1, SEG, HD), F32),
        pltpu.VMEM((tokens, HD), BF),
        pltpu.VMEM((2, 2, SIDE, SIDE, SEG, HD), BF),
        pltpu.VMEM((2, 2, 3, SIDE, SEG, HD), BF),
        pltpu.VMEM((2, 2, SIDE, SEG, HD), BF),
        pltpu.VMEM((2, 2, 3, SEG, HD), BF),
        pltpu.VMEM((2, 2, SIDE, SIDE, half, HD), BF),
        pltpu.VMEM((2, 2, 3, SIDE, half, HD), BF),
        pltpu.VMEM((2, 2, SIDE, half, HD), BF),
        pltpu.VMEM((2, 2, 3, half, HD), BF),
        pltpu.SemaphoreType.DMA((3,)),
        pltpu.SemaphoreType.DMA((2, 2, RANKS)),
        pltpu.SemaphoreType.DMA((2, 2, RANKS)),
        pltpu.SemaphoreType.DMA((4, 2, 2, SIDE)),
        pltpu.SemaphoreType.DMA((4, 2, 2, SIDE)),
    ]
    slots, where_to = pl.pallas_call(
        table_kernel,
        out_shape=(
            jax.ShapeDtypeStruct((2, DEPTH), jnp.int32),
            jax.ShapeDtypeStruct((2, SEGS), jnp.int32),
        ),
        in_specs=[smem],
        out_specs=(smem, smem),
    )(parents)
    return pl.pallas_call(
        kernel,
        out_shape=(
            jax.ShapeDtypeStruct((tokens, GROUP * HD), BF),
            jax.ShapeDtypeStruct((DCOLS, 2 * HD), F32),
        ),
        in_specs=[hbm, hbm, vmem, vmem, hbm, smem, smem],
        out_specs=(vmem, vmem),
        scratch_shapes=scratch,
        compiler_params=pltpu.CompilerParams(
            collective_id=1, has_side_effects=True, vmem_limit_bytes=60 << 20
        ),
    )(hidden_in, queries, keys, values, out_grad, slots, where_to)


def solution(mesh):
    rows = P(("leaf", "seq"), None)
    return jax.shard_map(
        on_device,
        mesh=mesh,
        in_specs=(rows, rows, rows, rows, rows, P("leaf")),
        out_specs=(rows, rows),
        check_vma=False,
    )
```

```python
import functools

import jax
import jax.numpy as jnp
from jax import lax
from jax.experimental import pallas as pl
from jax.experimental.pallas import tpu as pltpu
from jax.sharding import PartitionSpec as P

BF, F32 = jnp.bfloat16, jnp.float32
MESH = pl.DeviceIdType.MESH
SIDE = 4
RANKS = SIDE * SIDE
SEG, HD, GROUP = 128, 128, 8
SEGS = 2 * RANKS
DEPTH = 16
SLOTS = DEPTH + 1
KEYS = SLOTS * SEG
PAIRS = GROUP // 2
UNITS = 2 * PAIRS
W = 2 * SEG
MC = 544
D = 5120
DCOLS = D // RANKS
LOG2E = 1.4426950408889634
SCALE = HD ** -0.5
PEN = 1e30
STEPS = (1, 3, 2)


def dot(a, b):
    return jnp.dot(a, b, preferred_element_type=F32)


def place():
    me = lax.axis_index("seq")
    return me, me // SIDE, lax.rem(me, SIDE)


def at(dy, dx):
    _, y, x = place()
    return lax.rem(y + dy + SIDE, SIDE) * SIDE + lax.rem(x + dx + SIDE, SIDE)


def remote(src, dst, send, recv, rank):
    return pltpu.make_async_remote_copy(
        src, dst, send, recv, device_id={"seq": rank}, device_id_type=MESH
    )


def loop(count, body):
    def step(index, carry):
        body(index)
        return carry

    lax.fori_loop(0, count, step, 0)


def interleave(*parts):
    timed = [((i + 0.5) / len(part), n, i) for n, part in enumerate(parts) for i in range(len(part))]
    for _, n, i in sorted(timed):
        parts[n][i]()


def paired(first, second):
    interleave(first((0, 0)))

    def body(i):
        interleave(first((1, i)), second((0, i)))
        interleave(first((0, i + 1)), second((1, i)))

    loop(UNITS // 2 - 1, body)
    end = UNITS // 2 - 1
    interleave(first((1, end)), second((0, end)))
    interleave(second((1, end)))


def score_steps(unit, kc, qt, e, mxs):
    parity, index = unit
    u, t = 2 * index + parity, index // 2
    weights = qt[u]
    state = [jnp.full((8, W), -3e38, F32)]

    def step(start):
        s = dot(kc[t, pl.ds(start, MC), :], weights)
        if start + MC == KEYS:
            key = lax.broadcasted_iota(jnp.int32, (SEG, W), 0)
            row = lax.broadcasted_iota(jnp.int32, (SEG, W), 1)
            row = jnp.where(row >= SEG, row - SEG, row)
            own = jnp.where(key <= row, s[MC - SEG :], -PEN)
            s = jnp.concatenate([s[: MC - SEG], own], axis=0)
        e[parity][index, pl.ds(start, MC), :] = s
        state[0] = jnp.maximum(state[0], jnp.max(s.reshape(MC // 8, 8, W), axis=0))
        if start + MC == KEYS:
            mxs[u] = state[0]

    return [functools.partial(step, start) for start in range(0, KEYS, MC)]


def prob_steps(unit, slots, e, mxs, inv, p):
    parity, index = unit
    u, t = 2 * index + parity, index // 2
    m = jnp.max(mxs[u], axis=0, keepdims=True) * (SCALE * LOG2E)
    state = [jnp.zeros((8, W), F32), None]

    def power(i):
        rows = pl.ds(i * SEG, SEG)
        shift = m
        if i < DEPTH:
            shift = m + jnp.where(slots[t, i] == SEGS, jnp.float32(PEN), jnp.float32(0.0))
        x = jnp.exp2(e[parity][index, rows, :] * (SCALE * LOG2E) - shift)
        e[parity][index, rows, :] = x
        state[0] += jnp.sum(x.reshape(SEG // 8, 8, W), axis=0)

    def norm(i):
        rows = pl.ds(i * SEG, SEG)
        if i == 0:
            state[1] = 1.0 / jnp.sum(state[0], axis=0, keepdims=True)
            inv[u] = jnp.broadcast_to(state[1], (8, W))
        p[u, rows, :] = (e[parity][index, rows, :] * state[1]).astype(BF)

    return [functools.partial(f, i) for f in (power, norm) for i in range(SLOTS)]


def dprob_steps(unit, vc, gt, e, inv, dp, delta):
    parity, index = unit
    u, t = 2 * index + parity, index // 2
    weights = gt[u]
    state = [jnp.zeros((8, W), F32)]

    def step(start):
        rows = pl.ds(start, MC)
        x = dot(vc[t, rows, :], weights)
        dp[parity][rows, :] = x
        x = x * e[parity][index, rows, :]
        state[0] += jnp.sum(x.reshape(MC // 8, 8, W), axis=0)
        if start + MC == KEYS:
            total = jnp.sum(state[0], axis=0, keepdims=True) * inv[u, 0:1, :]
            delta[u] = jnp.broadcast_to(total, (8, W))

    return [functools.partial(step, start) for start in range(0, KEYS, MC)]


def dscore_steps(unit, e, inv, dp, delta, ds):
    parity, index = unit
    u = 2 * index + parity
    r = inv[u, 0:1, :]
    d = delta[u, 0:1, :]

    def step(i):
        rows = pl.ds(i * SEG, SEG)
        ds[u, rows, :] = (e[parity][index, rows, :] * r * (dp[parity][rows, :] - d)).astype(BF)

    return [functools.partial(step, i) for i in range(SLOTS)]


def side_grad(t, lhs, rhs, acc):
    total = dot(lhs[t * PAIRS], rhs[t * PAIRS])
    for h in range(1, PAIRS):
        total += dot(lhs[t * PAIRS + h], rhs[t * PAIRS + h])
    acc[t, pl.ds(0, SLOTS)] = total.reshape(SLOTS, SEG, HD)
    acc[t, SLOTS] = jnp.zeros((SEG, HD), F32)


def dq_unit(u, kct, ds, dq):
    t = u // PAIRS
    g = (dot(kct[t], ds[u]) * SCALE).T.astype(BF)
    first = lax.rem(u, PAIRS) * W
    rows = pl.ds(pl.multiple_of(t * SEG, SEG), SEG)
    for k in range(2):
        dq[rows, pl.ds(pl.multiple_of(first + k * HD, HD), HD)] = g[k * SEG : (k + 1) * SEG]


class Gather:
    def __init__(self, buf, send, recv):
        self.buf, self.send, self.recv = buf, send, recv
        self.copies = {}

    def shift(self, half, first, second):
        return at(second, first) if half == 0 else at(first, second)

    def start(self, half, p, q, to_p, to_q):
        origin = 2 * self.shift(half, -p, -q) + half
        target = self.shift(half, to_p - p, to_q - q)
        sem = (half, to_p * SIDE + to_q)
        copy = remote(
            self.buf.at[origin], self.buf.at[origin], self.send.at[sem], self.recv.at[sem], target
        )
        copy.start()
        self.copies[half, to_p, to_q] = copy

    def own(self):
        for step in STEPS:
            for half in range(2):
                self.start(half, 0, 0, step, 0)
        for step in STEPS:
            for half in range(2):
                self.start(half, 0, 0, 0, step)

    def forward(self):
        for p in STEPS:
            for half in range(2):
                self.copies[half, p, 0].wait_recv()
                for q in STEPS:
                    self.start(half, p, 0, p, q)

    def arrive(self):
        for (half, p, q), copy in self.copies.items():
            if q:
                copy.wait_recv()

    def drain(self):
        for copy in self.copies.values():
            copy.wait_send()


class Reduce:
    def __init__(self, stage, got, mid, last, send, recv):
        self.stage, self.got, self.mid, self.last = stage, got, mid, last
        self.send, self.recv = send, recv
        self.first, self.second = {}, {}

    def put(self, dest, low, high):
        y, x = dest // SIDE, lax.rem(dest, SIDE)
        self.stage[0, x, y] = low.astype(BF)
        self.stage[1, y, x] = high.astype(BF)

    def start(self):
        _, y, x = place()
        for step in STEPS:
            for half in range(2):
                column = lax.rem((x, y)[half] + step, SIDE)
                target = (at(0, step), at(step, 0))[half]
                self.first[half, step] = remote(
                    self.stage.at[half, column],
                    self.got.at[half, step - 1],
                    self.send.at[half, 0, step],
                    self.recv.at[half, 0, step],
                    target,
                )
                self.first[half, step].start()

    def middle(self):
        _, y, x = place()
        for half in range(2):
            for step in STEPS:
                self.first[half, step].wait_recv()
            here = (x, y)[half]
            for k in range(SIDE):
                total = self.stage[half, here, k].astype(F32)
                for step in STEPS:
                    total += self.got[half, step - 1, k].astype(F32)
                self.mid[half, k] = total.astype(BF)
            for step in STEPS:
                row = lax.rem((y, x)[half] + step, SIDE)
                target = (at(step, 0), at(0, step))[half]
                self.second[half, step] = remote(
                    self.mid.at[half, row],
                    self.last.at[half, step - 1],
                    self.send.at[half, 1, step],
                    self.recv.at[half, 1, step],
                    target,
                )
                self.second[half, step].start()

    def finish(self):
        _, y, x = place()
        totals = []
        for half in range(2):
            for step in STEPS:
                self.second[half, step].wait_recv()
            total = self.mid[half, (y, x)[half]].astype(F32)
            for step in STEPS:
                total += self.last[half, step - 1].astype(F32)
            totals.append(total)
        return totals

    def drain(self):
        for copy in [*self.first.values(), *self.second.values()]:
            copy.wait_send()


def table_kernel(parents, slots, where_to):
    me, _, _ = place()
    for t in range(2):
        cur = parents[2 * me + t]
        for i in range(DEPTH):
            slots[t, i] = jnp.where(cur >= 0, cur, SEGS)
            cur = jnp.where(cur >= 0, parents[jnp.maximum(cur, 0)], -1)

    def find(j):
        for t in range(2):
            found = jnp.where(j == 2 * me + t, DEPTH, SLOTS)
            for i in range(DEPTH):
                found = jnp.where(slots[t, i] == j, i, found)
            where_to[t, j] = found

    loop(SEGS, find)


def kernel(
    hid_ref, q_ref, k_ref, v_ref, g_ref, slots, where_to,
    dq_ref, proj_ref,
    hid_t, q, g, k_all, v_all, kc, vc, kct, qt, gt, qs, gs,
    e0, e1, dp0, dp1, p, mxs, inv, delta, side, low,
    kv_stage, kv_got, kv_mid, kv_last, pr_stage, pr_got, pr_mid, pr_last,
    local_sem, gather_send, gather_recv, sum_send, sum_recv,
):
    me, y, x = place()
    def park(c):
        return p.at[c % UNITS, pl.ds(c // UNITS * W, W), :]

    moves = [(q_ref, q), (g_ref, g)]
    moves += [(hid_ref.at[:, pl.ds(c * W, W)], park(c)) for c in range(D // W)]
    locals_ = [
        pltpu.make_async_copy(src, dst, local_sem.at[i]) for i, (src, dst) in enumerate(moves)
    ]
    for copy in locals_:
        copy.start()

    barrier = pltpu.get_barrier_semaphore()
    for step in STEPS:
        for mate in (at(0, step), at(step, 0)):
            pl.semaphore_signal(barrier, inc=1, device_id={"seq": mate}, device_id_type=MESH)
    for half in range(2):
        k_all[2 * me + half] = k_ref[half * SEG : (half + 1) * SEG, :]
        v_all[2 * me + half] = v_ref[half * SEG : (half + 1) * SEG, :]
    pl.semaphore_wait(barrier, 6)

    keys = Gather(k_all, gather_send.at[0], gather_recv.at[0])
    vals = Gather(v_all, gather_send.at[1], gather_recv.at[1])
    keys.own()

    locals_[0].wait()
    locals_[1].wait()

    def prepare(u):
        t = u // PAIRS
        first = lax.rem(u, PAIRS) * W
        rows = pl.ds(pl.multiple_of(t * SEG, SEG), SEG)
        for src, turned, stacked in ((q, qt, qs), (g, gt, gs)):
            for k in range(2):
                block = src[rows, pl.ds(pl.multiple_of(first + k * HD, HD), HD)]
                stacked[u, pl.ds(k * SEG, SEG), :] = block
                turned[u, :, pl.ds(k * SEG, SEG)] = block.T

    loop(UNITS, prepare)
    keys.forward()
    vals.own()
    vals.forward()

    for c in range(D // W):
        locals_[2 + c].wait()
        hid_t[pl.ds(c * W, W), :] = park(c)[...].T

    e, dp = (e0, e1), (dp0, dp1)
    keys.arrive()
    for t in range(2):
        head = k_all[2 * me + t, 0:16, :].astype(F32)[0:1]
        k_all[SEGS] = jnp.broadcast_to(head, (SEG, HD)).astype(BF)
        for i in range(SLOTS):
            block = k_all[slots[t, i]] if i < DEPTH else k_all[2 * me + t]
            kc[t, pl.ds(i * SEG, SEG), :] = block
            kct[t, :, pl.ds(i * SEG, SEG)] = block.T
    paired(
        lambda unit: score_steps(unit, kc, qt, e, mxs),
        lambda unit: prob_steps(unit, slots, e, mxs, inv, p),
    )

    def spread(acc, reduce):
        def put(dest):
            blocks = []
            for half in range(2):
                block = jnp.zeros((SEG, HD), F32)
                for t in range(2):
                    block += acc[t, where_to[t, 2 * dest + half]]
                blocks.append(block)
            reduce.put(dest, *blocks)

        loop(RANKS, put)
        reduce.start()

    def make(i, stage, got, mid, last):
        j = i % 2
        return Reduce(
            stage.at[j], got.at[j], mid.at[j], last.at[j], sum_send.at[i], sum_recv.at[i]
        )

    dv = make(0, kv_stage, kv_got, kv_mid, kv_last)
    dk = make(1, kv_stage, kv_got, kv_mid, kv_last)
    pv = make(2, pr_stage, pr_got, pr_mid, pr_last)
    pk = make(3, pr_stage, pr_got, pr_mid, pr_last)

    def project(reduce, grad, scale):
        for half, total in enumerate(grad.finish()):
            low[pl.ds(half * SEG, SEG), :] = (total * scale).astype(BF)
        weights = low[...]

        def put(dest):
            rows = pl.ds(pl.multiple_of(dest * DCOLS, 64), DCOLS)
            out = dot(hid_t[rows, :], weights)
            reduce.put(dest, out[: DCOLS // 2], out[DCOLS // 2 :])

        loop(RANKS, put)

    for t in range(2):
        side_grad(t, p, gs, side)
    spread(side, dv)

    vals.arrive()
    v_all[SEGS] = jnp.zeros((SEG, HD), BF)
    for t in range(2):
        for i in range(SLOTS):
            block = v_all[slots[t, i]] if i < DEPTH else v_all[2 * me + t]
            vc[t, pl.ds(i * SEG, SEG), :] = block
    paired(
        lambda unit: dprob_steps(unit, vc, gt, e, inv, dp, delta),
        lambda unit: dscore_steps(unit, e, inv, dp, delta, p),
    )
    dv.middle()
    for t in range(2):
        side_grad(t, p, qs, side)
    spread(side, dk)
    loop(UNITS, lambda u: dq_unit(u, kct, p, dq_ref))
    project(pv, dv, 1.0)
    dk.middle()
    pv.start()
    project(pk, dk, SCALE)
    pk.start()
    pv.middle()
    pk.middle()
    for half, total in enumerate(pv.finish()):
        proj_ref[pl.ds(half * (DCOLS // 2), DCOLS // 2), pl.ds(HD, HD)] = total
    for half, total in enumerate(pk.finish()):
        proj_ref[pl.ds(half * (DCOLS // 2), DCOLS // 2), pl.ds(0, HD)] = total
    for part in (keys, vals, dv, dk, pv, pk):
        part.drain()


def copy_kernel(dq_in, proj_in, dq_out, proj_out):
    dq_out[...] = dq_in[...]
    proj_out[...] = proj_in[...]


def on_device(hidden_in, queries, keys, values, out_grad, parents):
    vmem = pl.BlockSpec(memory_space=pltpu.VMEM)
    hbm = pl.BlockSpec(memory_space=pl.ANY)
    smem = pl.BlockSpec(memory_space=pltpu.SMEM)
    tokens = 2 * SEG
    half = DCOLS // 2
    scratch = [
        pltpu.VMEM((D, tokens), BF),
        pltpu.VMEM((tokens, GROUP * HD), BF),
        pltpu.VMEM((tokens, GROUP * HD), BF),
        pltpu.VMEM((SEGS + 1, SEG, HD), BF),
        pltpu.VMEM((SEGS + 1, SEG, HD), BF),
        pltpu.VMEM((2, KEYS, HD), BF),
        pltpu.VMEM((2, KEYS, HD), BF),
        pltpu.VMEM((2, HD, KEYS), BF),
        pltpu.VMEM((UNITS, HD, W), BF),
        pltpu.VMEM((UNITS, HD, W), BF),
        pltpu.VMEM((UNITS, W, HD), BF),
        pltpu.VMEM((UNITS, W, HD), BF),
        pltpu.VMEM((UNITS // 2, KEYS, W), F32),
        pltpu.VMEM((UNITS // 2, KEYS, W), F32),
        pltpu.VMEM((KEYS, W), F32),
        pltpu.VMEM((KEYS, W), F32),
        pltpu.VMEM((UNITS, KEYS, W), BF),
        pltpu.VMEM((UNITS, 8, W), F32),
        pltpu.VMEM((UNITS, 8, W), F32),
        pltpu.VMEM((UNITS, 8, W), F32),
        pltpu.VMEM((2, SLOTS + 1, SEG, HD), F32),
        pltpu.VMEM((tokens, HD), BF),
        pltpu.VMEM((2, 2, SIDE, SIDE, SEG, HD), BF),
        pltpu.VMEM((2, 2, 3, SIDE, SEG, HD), BF),
        pltpu.VMEM((2, 2, SIDE, SEG, HD), BF),
        pltpu.VMEM((2, 2, 3, SEG, HD), BF),
        pltpu.VMEM((2, 2, SIDE, SIDE, half, HD), BF),
        pltpu.VMEM((2, 2, 3, SIDE, half, HD), BF),
        pltpu.VMEM((2, 2, SIDE, half, HD), BF),
        pltpu.VMEM((2, 2, 3, half, HD), BF),
        pltpu.SemaphoreType.DMA((2 + D // W,)),
        pltpu.SemaphoreType.DMA((2, 2, RANKS)),
        pltpu.SemaphoreType.DMA((2, 2, RANKS)),
        pltpu.SemaphoreType.DMA((4, 2, 2, SIDE)),
        pltpu.SemaphoreType.DMA((4, 2, 2, SIDE)),
    ]
    slots, where_to = pl.pallas_call(
        table_kernel,
        out_shape=(
            jax.ShapeDtypeStruct((2, DEPTH), jnp.int32),
            jax.ShapeDtypeStruct((2, SEGS), jnp.int32),
        ),
        in_specs=[smem],
        out_specs=(smem, smem),
    )(parents)
    out_shape = (
        jax.ShapeDtypeStruct((tokens, GROUP * HD), BF),
        jax.ShapeDtypeStruct((DCOLS, 2 * HD), F32),
    )
    grads = pl.pallas_call(
        kernel,
        out_shape=out_shape,
        in_specs=[hbm, hbm, vmem, vmem, hbm, smem, smem],
        out_specs=(vmem, vmem),
        scratch_shapes=scratch,
        compiler_params=pltpu.CompilerParams(
            collective_id=1, has_side_effects=True, vmem_limit_bytes=62 << 20
        ),
    )(hidden_in, queries, keys, values, out_grad, slots, where_to)
    return pl.pallas_call(
        copy_kernel,
        out_shape=out_shape,
        in_specs=[vmem, vmem],
        out_specs=(vmem, vmem),
    )(*grads)


def solution(mesh):
    rows = P(("leaf", "seq"), None)
    return jax.shard_map(
        on_device,
        mesh=mesh,
        in_specs=(rows, rows, rows, rows, rows, P("leaf")),
        out_specs=(rows, rows),
        check_vma=False,
    )
```

```python
import functools

import jax
import jax.numpy as jnp
from jax import lax
from jax.experimental import pallas as pl
from jax.experimental.pallas import tpu as pltpu
from jax.sharding import PartitionSpec as P

BF, F32 = jnp.bfloat16, jnp.float32
MESH = pl.DeviceIdType.MESH
SIDE = 4
RANKS = SIDE * SIDE
SEG, HD, GROUP = 128, 128, 8
SEGS = 2 * RANKS
DEPTH = 16
SLOTS = DEPTH + 1
KEYS = SLOTS * SEG
PAIRS = GROUP // 2
UNITS = 2 * PAIRS
W = 2 * SEG
MC = 544
D = 5120
DCOLS = D // RANKS
LOG2E = 1.4426950408889634
SCALE = HD ** -0.5
PEN = 1e30
STEPS = (1, 3, 2)


def dot(a, b):
    return jnp.dot(a, b, preferred_element_type=F32)


def place():
    me = lax.axis_index("seq")
    return me, me // SIDE, lax.rem(me, SIDE)


def at(dy, dx):
    _, y, x = place()
    return lax.rem(y + dy + SIDE, SIDE) * SIDE + lax.rem(x + dx + SIDE, SIDE)


def remote(src, dst, send, recv, rank):
    return pltpu.make_async_remote_copy(
        src, dst, send, recv, device_id={"seq": rank}, device_id_type=MESH
    )


def loop(count, body):
    def step(index, carry):
        body(index)
        return carry

    lax.fori_loop(0, count, step, 0)


def interleave(*parts):
    timed = [((i + 0.5) / len(part), n, i) for n, part in enumerate(parts) for i in range(len(part))]
    for _, n, i in sorted(timed):
        parts[n][i]()


def paired(first, second):
    interleave(first((0, 0)))

    def body(i):
        interleave(first((1, i)), second((0, i)))
        interleave(first((0, i + 1)), second((1, i)))

    loop(UNITS // 2 - 1, body)
    end = UNITS // 2 - 1
    interleave(first((1, end)), second((0, end)))
    interleave(second((1, end)))


def score_steps(unit, kc, qt, e, mxs):
    parity, index = unit
    u, t = 2 * index + parity, index // 2
    weights = qt[u]
    state = [jnp.full((8, W), -3e38, F32)]

    def step(start):
        s = dot(kc[t, pl.ds(start, MC), :], weights)
        if start + MC == KEYS:
            key = lax.broadcasted_iota(jnp.int32, (SEG, W), 0)
            row = lax.broadcasted_iota(jnp.int32, (SEG, W), 1)
            row = jnp.where(row >= SEG, row - SEG, row)
            own = jnp.where(key <= row, s[MC - SEG :], -PEN)
            s = jnp.concatenate([s[: MC - SEG], own], axis=0)
        e[parity][index, pl.ds(start, MC), :] = s
        state[0] = jnp.maximum(state[0], jnp.max(s.reshape(MC // 8, 8, W), axis=0))
        if start + MC == KEYS:
            mxs[u] = state[0]

    return [functools.partial(step, start) for start in range(0, KEYS, MC)]


def prob_steps(unit, slots, e, mxs, inv, p):
    parity, index = unit
    u, t = 2 * index + parity, index // 2
    m = jnp.max(mxs[u], axis=0, keepdims=True) * (SCALE * LOG2E)
    state = [jnp.zeros((8, W), F32), None]

    def power(i):
        rows = pl.ds(i * SEG, SEG)
        shift = m
        if i < DEPTH:
            shift = m + jnp.where(slots[t, i] == SEGS, jnp.float32(PEN), jnp.float32(0.0))
        x = jnp.exp2(e[parity][index, rows, :] * (SCALE * LOG2E) - shift)
        e[parity][index, rows, :] = x
        state[0] += jnp.sum(x.reshape(SEG // 8, 8, W), axis=0)

    def norm(i):
        rows = pl.ds(i * SEG, SEG)
        if i == 0:
            state[1] = 1.0 / jnp.sum(state[0], axis=0, keepdims=True)
            inv[u] = jnp.broadcast_to(state[1], (8, W))
        p[u, rows, :] = (e[parity][index, rows, :] * state[1]).astype(BF)

    return [functools.partial(f, i) for f in (power, norm) for i in range(SLOTS)]


def dprob_steps(unit, vc, gt, e, inv, dp, delta):
    parity, index = unit
    u, t = 2 * index + parity, index // 2
    weights = gt[u]
    state = [jnp.zeros((8, W), F32)]

    def step(start):
        rows = pl.ds(start, MC)
        x = dot(vc[t, rows, :], weights)
        dp[parity][rows, :] = x
        x = x * e[parity][index, rows, :]
        state[0] += jnp.sum(x.reshape(MC // 8, 8, W), axis=0)
        if start + MC == KEYS:
            total = jnp.sum(state[0], axis=0, keepdims=True) * inv[u, 0:1, :]
            delta[u] = jnp.broadcast_to(total, (8, W))

    return [functools.partial(step, start) for start in range(0, KEYS, MC)]


def dscore_steps(unit, e, inv, dp, delta, ds):
    parity, index = unit
    u = 2 * index + parity
    r = inv[u, 0:1, :]
    d = delta[u, 0:1, :]

    def step(i):
        rows = pl.ds(i * SEG, SEG)
        ds[u, rows, :] = (e[parity][index, rows, :] * r * (dp[parity][rows, :] - d)).astype(BF)

    return [functools.partial(step, i) for i in range(SLOTS)]


def side_grad(t, lhs, rhs, acc):
    total = dot(lhs[t * PAIRS], rhs[t * PAIRS])
    for h in range(1, PAIRS):
        total += dot(lhs[t * PAIRS + h], rhs[t * PAIRS + h])
    acc[t, pl.ds(0, SLOTS)] = total.reshape(SLOTS, SEG, HD)
    acc[t, SLOTS] = jnp.zeros((SEG, HD), F32)


def dq_unit(u, kct, ds, dq):
    t = u // PAIRS
    g = (dot(kct[t], ds[u]) * SCALE).T.astype(BF)
    first = lax.rem(u, PAIRS) * W
    rows = pl.ds(pl.multiple_of(t * SEG, SEG), SEG)
    for k in range(2):
        dq[rows, pl.ds(pl.multiple_of(first + k * HD, HD), HD)] = g[k * SEG : (k + 1) * SEG]


class Gather:
    def __init__(self, buf, send, recv):
        self.buf, self.send, self.recv = buf, send, recv
        self.copies = {}

    def shift(self, half, first, second):
        return at(second, first) if half == 0 else at(first, second)

    def start(self, half, p, q, to_p, to_q):
        origin = 2 * self.shift(half, -p, -q) + half
        target = self.shift(half, to_p - p, to_q - q)
        sem = (half, to_p * SIDE + to_q)
        copy = remote(
            self.buf.at[origin], self.buf.at[origin], self.send.at[sem], self.recv.at[sem], target
        )
        copy.start()
        self.copies[half, to_p, to_q] = copy

    def own(self):
        for step in STEPS:
            for half in range(2):
                self.start(half, 0, 0, step, 0)
        for step in STEPS:
            for half in range(2):
                self.start(half, 0, 0, 0, step)

    def forward(self):
        for p in STEPS:
            for half in range(2):
                self.copies[half, p, 0].wait_recv()
                for q in STEPS:
                    self.start(half, p, 0, p, q)

    def arrive(self):
        for (half, p, q), copy in self.copies.items():
            if q:
                copy.wait_recv()

    def drain(self):
        for copy in self.copies.values():
            copy.wait_send()


class Reduce:
    def __init__(self, stage, own, got, mid, last, send, recv, send_on, recv_on):
        self.stage, self.own, self.got, self.mid, self.last = stage, own, got, mid, last
        self.send, self.recv, self.send_on, self.recv_on = send, recv, send_on, recv_on
        self.first, self.second = {}, {}

    def scatter(self, block, now=True):
        _, y, x = place()
        for step in (*STEPS, 0):
            for half in range(2):
                mine, other = ((x, y), (y, x))[half]
                column = lax.rem(mine + step, SIDE)
                for j in range(SIDE):
                    k = lax.rem(other + 1 + j, SIDE)
                    rank = k * SIDE + column if half == 0 else column * SIDE + k
                    value = block(rank, half)
                    if step == 0:
                        self.own[half, k] = value
                        continue
                    self.stage[half, step - 1, k] = value.astype(BF)
                    copy = remote(
                        self.stage.at[half, step - 1, k],
                        self.got.at[half, step - 1, k],
                        self.send.at[half, step, j],
                        self.recv.at[half, step, j],
                        (at(0, step), at(step, 0))[half],
                    )
                    self.first[half, step, j] = copy
                    if now:
                        copy.start()

    def start(self):
        for copy in self.first.values():
            copy.start()

    def middle(self):
        _, y, x = place()
        for j in range(SIDE):
            for half in range(2):
                k = lax.rem((y, x)[half] + 1 + j, SIDE)
                for step in STEPS:
                    self.first[half, step, j].wait_recv()
                total = self.own[half, k]
                for step in STEPS:
                    total += self.got[half, step - 1, k].astype(F32)
                if j == SIDE - 1:
                    self.own[half, k] = total
                    continue
                self.mid[half, j] = total.astype(BF)
                copy = remote(
                    self.mid.at[half, j],
                    self.last.at[half, j],
                    self.send_on.at[half, j],
                    self.recv_on.at[half, j],
                    (at(j + 1, 0), at(0, j + 1))[half],
                )
                copy.start()
                self.second[half, j] = copy

    def finish(self, half):
        _, y, x = place()
        total = self.own[half, (y, x)[half]]
        for j in range(SIDE - 1):
            self.second[half, j].wait_recv()
            total += self.last[half, j].astype(F32)
        return total

    def drain(self):
        for copy in [*self.first.values(), *self.second.values()]:
            copy.wait_send()


def kernel(
    hid_ref, q_ref, k_ref, v_ref, g_ref, parents,
    dq_ref, proj_ref,
    hid_t, q, g, k_all, v_all, kc, vc, kct, qt, gt, qs, gs,
    e0, e1, dp0, dp1, p, mxs, inv, delta, side, low,
    kv_stage, kv_own, kv_got, kv_mid, kv_last, pr_stage, pr_own, pr_got, pr_mid, pr_last,
    slots, where_to, local_sem, gather_send, gather_recv,
    sum_send, sum_recv, sum_send_on, sum_recv_on,
):
    me, y, x = place()
    def park(c):
        return p.at[c % UNITS, pl.ds(c // UNITS * W, W), :]

    moves = [(q_ref, q), (g_ref, g)]
    moves += [(hid_ref.at[:, pl.ds(c * W, W)], park(c)) for c in range(D // W)]
    locals_ = [
        pltpu.make_async_copy(src, dst, local_sem.at[i]) for i, (src, dst) in enumerate(moves)
    ]
    for copy in locals_:
        copy.start()

    barrier = pltpu.get_barrier_semaphore()
    for step in STEPS:
        for mate in (at(0, step), at(step, 0)):
            pl.semaphore_signal(barrier, inc=1, device_id={"seq": mate}, device_id_type=MESH)
    for half in range(2):
        k_all[2 * me + half] = k_ref[half * SEG : (half + 1) * SEG, :]
        v_all[2 * me + half] = v_ref[half * SEG : (half + 1) * SEG, :]
    pl.semaphore_wait(barrier, 6)

    keys = Gather(k_all, gather_send.at[0], gather_recv.at[0])
    vals = Gather(v_all, gather_send.at[1], gather_recv.at[1])
    keys.own()

    for t in range(2):
        cur = parents[2 * me + t]
        for i in range(DEPTH):
            slots[t, i] = jnp.where(cur >= 0, cur, SEGS)
            cur = jnp.where(cur >= 0, parents[jnp.maximum(cur, 0)], -1)

    def find(j):
        for t in range(2):
            found = jnp.where(j == 2 * me + t, DEPTH, SLOTS)
            for i in range(DEPTH):
                found = jnp.where(slots[t, i] == j, i, found)
            where_to[t, j] = found

    loop(SEGS, find)

    locals_[0].wait()
    locals_[1].wait()

    def prepare(u):
        t = u // PAIRS
        first = lax.rem(u, PAIRS) * W
        rows = pl.ds(pl.multiple_of(t * SEG, SEG), SEG)
        for src, turned, stacked in ((q, qt, qs), (g, gt, gs)):
            for k in range(2):
                block = src[rows, pl.ds(pl.multiple_of(first + k * HD, HD), HD)]
                stacked[u, pl.ds(k * SEG, SEG), :] = block
                turned[u, :, pl.ds(k * SEG, SEG)] = block.T

    loop(UNITS, prepare)
    keys.forward()
    vals.own()
    vals.forward()

    for c in range(D // W):
        locals_[2 + c].wait()
        hid_t[pl.ds(c * W, W), :] = park(c)[...].T

    e, dp = (e0, e1), (dp0, dp1)
    keys.arrive()
    for t in range(2):
        head = k_all[2 * me + t, 0:16, :].astype(F32)[0:1]
        k_all[SEGS] = jnp.broadcast_to(head, (SEG, HD)).astype(BF)
        for i in range(SLOTS):
            block = k_all[slots[t, i]] if i < DEPTH else k_all[2 * me + t]
            kc[t, pl.ds(i * SEG, SEG), :] = block
            kct[t, :, pl.ds(i * SEG, SEG)] = block.T
    paired(
        lambda unit: score_steps(unit, kc, qt, e, mxs),
        lambda unit: prob_steps(unit, slots, e, mxs, inv, p),
    )

    def make(i, *buffers):
        sems = (sum_send, sum_recv, sum_send_on, sum_recv_on)
        return Reduce(*(b.at[i % 2] for b in buffers), *(sem.at[i] for sem in sems))

    dv = make(0, kv_stage, kv_own, kv_got, kv_mid, kv_last)
    dk = make(1, kv_stage, kv_own, kv_got, kv_mid, kv_last)
    pv = make(2, pr_stage, pr_own, pr_got, pr_mid, pr_last)
    pk = make(3, pr_stage, pr_own, pr_got, pr_mid, pr_last)

    def side_block(rank, half):
        segment = 2 * rank + half
        return side[0, where_to[0, segment]] + side[1, where_to[1, segment]]

    def project(reduce, grad, scale, now):
        for half in range(2):
            low[pl.ds(half * SEG, SEG), :] = (grad.finish(half) * scale).astype(BF)
        weights = low[...]

        def block(rank, half):
            first = rank * DCOLS + half * (DCOLS // 2)
            return dot(hid_t[pl.ds(pl.multiple_of(first, 32), DCOLS // 2), :], weights)

        reduce.scatter(block, now)

    for t in range(2):
        side_grad(t, p, gs, side)
    dv.scatter(side_block)

    vals.arrive()
    v_all[SEGS] = jnp.zeros((SEG, HD), BF)
    for t in range(2):
        for i in range(SLOTS):
            block = v_all[slots[t, i]] if i < DEPTH else v_all[2 * me + t]
            vc[t, pl.ds(i * SEG, SEG), :] = block
    paired(
        lambda unit: dprob_steps(unit, vc, gt, e, inv, dp, delta),
        lambda unit: dscore_steps(unit, e, inv, dp, delta, p),
    )
    dv.middle()
    for t in range(2):
        side_grad(t, p, qs, side)
    dk.scatter(side_block)
    loop(UNITS, lambda u: dq_unit(u, kct, p, dq_ref))
    project(pv, dv, 1.0, False)
    dk.middle()
    pv.start()
    project(pk, dk, SCALE, True)
    pv.middle()
    pk.middle()
    for half in range(2):
        rows = pl.ds(half * (DCOLS // 2), DCOLS // 2)
        proj_ref[rows, pl.ds(HD, HD)] = pv.finish(half)
        proj_ref[rows, pl.ds(0, HD)] = pk.finish(half)
    for part in (keys, vals, dv, dk, pv, pk):
        part.drain()


def copy_kernel(dq_in, proj_in, dq_out, proj_out):
    dq_out[...] = dq_in[...]
    proj_out[...] = proj_in[...]


def on_device(hidden_in, queries, keys, values, out_grad, parents):
    vmem = pl.BlockSpec(memory_space=pltpu.VMEM)
    hbm = pl.BlockSpec(memory_space=pl.ANY)
    smem = pl.BlockSpec(memory_space=pltpu.SMEM)
    tokens = 2 * SEG
    half = DCOLS // 2
    scratch = [
        pltpu.VMEM((D, tokens), BF),
        pltpu.VMEM((tokens, GROUP * HD), BF),
        pltpu.VMEM((tokens, GROUP * HD), BF),
        pltpu.VMEM((SEGS + 1, SEG, HD), BF),
        pltpu.VMEM((SEGS + 1, SEG, HD), BF),
        pltpu.VMEM((2, KEYS, HD), BF),
        pltpu.VMEM((2, KEYS, HD), BF),
        pltpu.VMEM((2, HD, KEYS), BF),
        pltpu.VMEM((UNITS, HD, W), BF),
        pltpu.VMEM((UNITS, HD, W), BF),
        pltpu.VMEM((UNITS, W, HD), BF),
        pltpu.VMEM((UNITS, W, HD), BF),
        pltpu.VMEM((UNITS // 2, KEYS, W), F32),
        pltpu.VMEM((UNITS // 2, KEYS, W), F32),
        pltpu.VMEM((KEYS, W), F32),
        pltpu.VMEM((KEYS, W), F32),
        pltpu.VMEM((UNITS, KEYS, W), BF),
        pltpu.VMEM((UNITS, 8, W), F32),
        pltpu.VMEM((UNITS, 8, W), F32),
        pltpu.VMEM((UNITS, 8, W), F32),
        pltpu.VMEM((2, SLOTS + 1, SEG, HD), F32),
        pltpu.VMEM((tokens, HD), BF),
        pltpu.VMEM((2, 2, SIDE - 1, SIDE, SEG, HD), BF),
        pltpu.VMEM((2, 2, SIDE, SEG, HD), F32),
        pltpu.VMEM((2, 2, SIDE - 1, SIDE, SEG, HD), BF),
        pltpu.VMEM((2, 2, SIDE - 1, SEG, HD), BF),
        pltpu.VMEM((2, 2, SIDE - 1, SEG, HD), BF),
        pltpu.VMEM((2, 2, SIDE - 1, SIDE, half, HD), BF),
        pltpu.VMEM((2, 2, SIDE, half, HD), F32),
        pltpu.VMEM((2, 2, SIDE - 1, SIDE, half, HD), BF),
        pltpu.VMEM((2, 2, SIDE - 1, half, HD), BF),
        pltpu.VMEM((2, 2, SIDE - 1, half, HD), BF),
        pltpu.SMEM((2, DEPTH), jnp.int32),
        pltpu.SMEM((2, SEGS), jnp.int32),
        pltpu.SemaphoreType.DMA((2 + D // W,)),
        pltpu.SemaphoreType.DMA((2, 2, RANKS)),
        pltpu.SemaphoreType.DMA((2, 2, RANKS)),
        pltpu.SemaphoreType.DMA((4, 2, SIDE, SIDE)),
        pltpu.SemaphoreType.DMA((4, 2, SIDE, SIDE)),
        pltpu.SemaphoreType.DMA((4, 2, SIDE)),
        pltpu.SemaphoreType.DMA((4, 2, SIDE)),
    ]
    out_shape = (
        jax.ShapeDtypeStruct((tokens, GROUP * HD), BF),
        jax.ShapeDtypeStruct((DCOLS, 2 * HD), F32),
    )
    grads = pl.pallas_call(
        kernel,
        out_shape=out_shape,
        in_specs=[hbm, hbm, vmem, vmem, hbm, smem],
        out_specs=(vmem, vmem),
        scratch_shapes=scratch,
        compiler_params=pltpu.CompilerParams(
            collective_id=1, has_side_effects=True, vmem_limit_bytes=62 << 20
        ),
    )(hidden_in, queries, keys, values, out_grad, parents)
    return pl.pallas_call(
        copy_kernel,
        out_shape=out_shape,
        in_specs=[vmem, vmem],
        out_specs=(vmem, vmem),
    )(*grads)


def solution(mesh):
    rows = P(("leaf", "seq"), None)
    return jax.shard_map(
        on_device,
        mesh=mesh,
        in_specs=(rows, rows, rows, rows, rows, P("leaf")),
        out_specs=(rows, rows),
        check_vma=False,
    )
```

```python
import functools

import jax
import jax.numpy as jnp
from jax import lax
from jax.experimental import pallas as pl
from jax.experimental.pallas import tpu as pltpu
from jax.sharding import PartitionSpec as P

BF, F32 = jnp.bfloat16, jnp.float32
MESH = pl.DeviceIdType.MESH
SIDE = 4
RANKS = SIDE * SIDE
SEG, HD, GROUP = 128, 128, 8
SEGS = 2 * RANKS
DEPTH = 16
SLOTS = DEPTH + 1
KEYS = SLOTS * SEG
PAIRS = GROUP // 2
UNITS = 2 * PAIRS
W = 2 * SEG
MC = 544
D = 5120
DCOLS = D // RANKS
LOG2E = 1.4426950408889634
SCALE = HD ** -0.5
PEN = 1e30
STEPS = (1, 3, 2)


def dot(a, b):
    return jnp.dot(a, b, preferred_element_type=F32)


def place():
    me = lax.axis_index("seq")
    return me, me // SIDE, lax.rem(me, SIDE)


def at(dy, dx):
    _, y, x = place()
    return lax.rem(y + dy + SIDE, SIDE) * SIDE + lax.rem(x + dx + SIDE, SIDE)


def remote(src, dst, send, recv, rank):
    return pltpu.make_async_remote_copy(
        src, dst, send, recv, device_id={"seq": rank}, device_id_type=MESH
    )


def loop(count, body):
    def step(index, carry):
        body(index)
        return carry

    lax.fori_loop(0, count, step, 0)


def interleave(*parts):
    timed = [((i + 0.5) / len(part), n, i) for n, part in enumerate(parts) for i in range(len(part))]
    for _, n, i in sorted(timed):
        parts[n][i]()


def paired(first, second):
    interleave(first((0, 0)))

    def body(i):
        interleave(first((1, i)), second((0, i)))
        interleave(first((0, i + 1)), second((1, i)))

    loop(UNITS // 2 - 1, body)
    end = UNITS // 2 - 1
    interleave(first((1, end)), second((0, end)))
    interleave(second((1, end)))


def score_steps(unit, kc, qt, e, mxs):
    parity, index = unit
    u, t = 2 * index + parity, index // 2
    weights = qt[u]
    state = [jnp.full((8, W), -3e38, F32)]

    def step(start):
        s = dot(kc[t, pl.ds(start, MC), :], weights)
        if start + MC == KEYS:
            key = lax.broadcasted_iota(jnp.int32, (SEG, W), 0)
            row = lax.broadcasted_iota(jnp.int32, (SEG, W), 1)
            row = jnp.where(row >= SEG, row - SEG, row)
            own = jnp.where(key <= row, s[MC - SEG :], -PEN)
            s = jnp.concatenate([s[: MC - SEG], own], axis=0)
        e[parity][index, pl.ds(start, MC), :] = s
        state[0] = jnp.maximum(state[0], jnp.max(s.reshape(MC // 8, 8, W), axis=0))
        if start + MC == KEYS:
            mxs[u] = state[0]

    return [functools.partial(step, start) for start in range(0, KEYS, MC)]


def prob_steps(unit, slots, e, mxs, inv, p):
    parity, index = unit
    u, t = 2 * index + parity, index // 2
    m = jnp.max(mxs[u], axis=0, keepdims=True) * (SCALE * LOG2E)
    state = [jnp.zeros((8, W), F32), None]

    def power(i):
        rows = pl.ds(i * SEG, SEG)
        shift = m
        if i < DEPTH:
            shift = m + jnp.where(slots[t, i] == SEGS, jnp.float32(PEN), jnp.float32(0.0))
        x = jnp.exp2(e[parity][index, rows, :] * (SCALE * LOG2E) - shift)
        e[parity][index, rows, :] = x
        state[0] += jnp.sum(x.reshape(SEG // 8, 8, W), axis=0)

    def norm(i):
        rows = pl.ds(i * SEG, SEG)
        if i == 0:
            state[1] = 1.0 / jnp.sum(state[0], axis=0, keepdims=True)
            inv[u] = jnp.broadcast_to(state[1], (8, W))
        p[u, rows, :] = (e[parity][index, rows, :] * state[1]).astype(BF)

    return [functools.partial(f, i) for f in (power, norm) for i in range(SLOTS)]


def dprob_steps(unit, vc, gt, e, inv, dp, delta):
    parity, index = unit
    u, t = 2 * index + parity, index // 2
    weights = gt[u]
    state = [jnp.zeros((8, W), F32)]

    def step(start):
        rows = pl.ds(start, MC)
        x = dot(vc[t, rows, :], weights)
        dp[parity][rows, :] = x
        x = x * e[parity][index, rows, :]
        state[0] += jnp.sum(x.reshape(MC // 8, 8, W), axis=0)
        if start + MC == KEYS:
            total = jnp.sum(state[0], axis=0, keepdims=True) * inv[u, 0:1, :]
            delta[u] = jnp.broadcast_to(total, (8, W))

    return [functools.partial(step, start) for start in range(0, KEYS, MC)]


def dscore_steps(unit, e, inv, dp, delta, ds):
    parity, index = unit
    u = 2 * index + parity
    r = inv[u, 0:1, :]
    d = delta[u, 0:1, :]

    def step(i):
        rows = pl.ds(i * SEG, SEG)
        ds[u, rows, :] = (e[parity][index, rows, :] * r * (dp[parity][rows, :] - d)).astype(BF)

    return [functools.partial(step, i) for i in range(SLOTS)]


def side_grad(t, lhs, rhs, acc):
    total = dot(lhs[t * PAIRS], rhs[t * PAIRS])
    for h in range(1, PAIRS):
        total += dot(lhs[t * PAIRS + h], rhs[t * PAIRS + h])
    acc[t, pl.ds(0, SLOTS)] = total.reshape(SLOTS, SEG, HD)
    acc[t, SLOTS] = jnp.zeros((SEG, HD), F32)


def dq_unit(u, kct, ds, dq):
    t = u // PAIRS
    g = (dot(kct[t], ds[u]) * SCALE).T.astype(BF)
    first = lax.rem(u, PAIRS) * W
    rows = pl.ds(pl.multiple_of(t * SEG, SEG), SEG)
    for k in range(2):
        dq[rows, pl.ds(pl.multiple_of(first + k * HD, HD), HD)] = g[k * SEG : (k + 1) * SEG]


class Gather:
    def __init__(self, buf, send, recv):
        self.buf, self.send, self.recv = buf, send, recv
        self.copies = {}

    def shift(self, half, first, second):
        return at(second, first) if half == 0 else at(first, second)

    def start(self, half, p, q, to_p, to_q):
        origin = 2 * self.shift(half, -p, -q) + half
        target = self.shift(half, to_p - p, to_q - q)
        sem = (half, to_p * SIDE + to_q)
        copy = remote(
            self.buf.at[origin], self.buf.at[origin], self.send.at[sem], self.recv.at[sem], target
        )
        copy.start()
        self.copies[half, to_p, to_q] = copy

    def own(self):
        for step in STEPS:
            for half in range(2):
                self.start(half, 0, 0, step, 0)
        for step in STEPS:
            for half in range(2):
                self.start(half, 0, 0, 0, step)

    def forward(self):
        for p in STEPS:
            for half in range(2):
                self.copies[half, p, 0].wait_recv()
                for q in STEPS:
                    self.start(half, p, 0, p, q)

    def arrive(self):
        for (half, p, q), copy in self.copies.items():
            if q:
                copy.wait_recv()

    def drain(self):
        for copy in self.copies.values():
            copy.wait_send()


class Reduce:
    def __init__(self, stage, own, got, mid, last, send, recv, send_on, recv_on):
        self.stage, self.own, self.got, self.mid, self.last = stage, own, got, mid, last
        self.send, self.recv, self.send_on, self.recv_on = send, recv, send_on, recv_on
        self.first, self.second = {}, {}

    def scatter(self, block):
        _, y, x = place()
        for step in (*STEPS, 0):
            for half in range(2):
                mine, other = ((x, y), (y, x))[half]
                column = lax.rem(mine + step, SIDE)
                for j in range(SIDE):
                    k = lax.rem(other + 1 + j, SIDE)
                    rank = k * SIDE + column if half == 0 else column * SIDE + k
                    value = block(rank, half)
                    if step == 0:
                        self.own[half, k] = value
                        continue
                    self.stage[half, step - 1, k] = value.astype(BF)
                    copy = remote(
                        self.stage.at[half, step - 1, k],
                        self.got.at[half, step - 1, k],
                        self.send.at[half, step, j],
                        self.recv.at[half, step, j],
                        (at(0, step), at(step, 0))[half],
                    )
                    copy.start()
                    self.first[half, step, j] = copy

    def total(self, half, j, k):
        for step in STEPS:
            self.first[half, step, j].wait_recv()
        total = self.own[half, k]
        for step in STEPS:
            total += self.got[half, step - 1, k].astype(F32)
        return total

    def middle(self):
        _, y, x = place()
        for j in range(SIDE):
            for half in range(2):
                k = lax.rem((y, x)[half] + 1 + j, SIDE)
                total = self.total(half, j, k)
                if j == SIDE - 1:
                    self.own[half, k] = total
                    continue
                self.mid[half, j] = total.astype(BF)
                copy = remote(
                    self.mid.at[half, j],
                    self.last.at[half, j],
                    self.send_on.at[half, j],
                    self.recv_on.at[half, j],
                    (at(j + 1, 0), at(0, j + 1))[half],
                )
                copy.start()
                self.second[half, j] = copy

    def finish(self, half):
        _, y, x = place()
        total = self.own[half, (y, x)[half]]
        for j in range(SIDE - 1):
            self.second[half, j].wait_recv()
            total += self.last[half, j].astype(F32)
        return total

    def drain(self):
        for copy in [*self.first.values(), *self.second.values()]:
            copy.wait_send()


class Hidden:
    def __init__(self, hid_t, got, send, recv):
        self.hid_t, self.got, self.send, self.recv = hid_t, got, send, recv
        self.copies, self.here = {}, set()

    def rows(self, column, k, half):
        rank = k * SIDE + column if half == 0 else column * SIDE + k
        first = rank * DCOLS + half * (DCOLS // 2)
        return pl.ds(pl.multiple_of(first, 32), DCOLS // 2)

    def start(self):
        _, y, x = place()
        for step in STEPS:
            for half in range(2):
                mine, other = ((x, y), (y, x))[half]
                for j in range(SIDE):
                    k = lax.rem(other + 1 + j, SIDE)
                    copy = remote(
                        self.hid_t.at[self.rows(lax.rem(mine + step, SIDE), k, half), :],
                        self.got.at[half, step - 1, k],
                        self.send.at[half, step, j],
                        self.recv.at[half, step, j],
                        (at(0, step), at(step, 0))[half],
                    )
                    copy.start()
                    self.copies[half, step, j] = copy

    def blocks(self, half, j, k):
        _, y, x = place()
        if (half, j) not in self.here:
            self.here.add((half, j))
            for step in STEPS:
                self.copies[half, step, j].wait_recv()
        own = self.hid_t[self.rows((x, y)[half], k, half), :]
        return [own, *(self.got[half, step - 1, k] for step in STEPS)]

    def drain(self):
        for copy in self.copies.values():
            copy.wait_send()


class Project(Reduce):
    def __init__(self, hidden, low, low_got, share_send, share_recv, own, mid, last, *sems):
        super().__init__(None, own, None, mid, last, None, None, *sems)
        self.hidden, self.low, self.low_got = hidden, low, low_got
        self.share_send, self.share_recv = share_send, share_recv

    def share(self, grad, scale):
        for half in range(2):
            self.low[pl.ds(half * SEG, SEG), :] = (grad.finish(half) * scale).astype(BF)
        for step in STEPS:
            for half in range(2):
                copy = remote(
                    self.low,
                    self.low_got.at[half, step - 1],
                    self.share_send.at[half, step],
                    self.share_recv.at[half, step],
                    (at(0, step), at(step, 0))[half],
                )
                copy.start()
                self.first[half, step] = copy

    def total(self, half, j, k):
        if j == 0:
            for step in STEPS:
                self.first[half, step].wait_recv()
        blocks = self.hidden.blocks(half, j, k)
        total = dot(blocks[0], self.low[...])
        for step, block in zip(STEPS, blocks[1:]):
            total += dot(block, self.low_got[half, step - 1])
        return total


def kernel(
    hid_ref, q_ref, k_ref, v_ref, g_ref, parents,
    dq_ref, proj_ref,
    hid_t, q, g, k_all, v_all, kc, vc, kct, qt, gt, qs, gs,
    e0, e1, dp0, dp1, p, mxs, inv, delta, side, low, low_got,
    kv_stage, kv_own, kv_got, kv_mid, kv_last, hid_got, pr_own, pr_mid, pr_last,
    slots, where_to, local_sem, gather_send, gather_recv,
    sum_send, sum_recv, sum_send_on, sum_recv_on,
    hid_send, hid_recv, share_send, share_recv,
):
    me, y, x = place()
    def park(c):
        return p.at[c % UNITS, pl.ds(c // UNITS * W, W), :]

    moves = [(q_ref, q), (g_ref, g)]
    moves += [(hid_ref.at[:, pl.ds(c * W, W)], park(c)) for c in range(D // W)]
    locals_ = [
        pltpu.make_async_copy(src, dst, local_sem.at[i]) for i, (src, dst) in enumerate(moves)
    ]
    for copy in locals_:
        copy.start()

    barrier = pltpu.get_barrier_semaphore()
    for step in STEPS:
        for mate in (at(0, step), at(step, 0)):
            pl.semaphore_signal(barrier, inc=1, device_id={"seq": mate}, device_id_type=MESH)
    for half in range(2):
        k_all[2 * me + half] = k_ref[half * SEG : (half + 1) * SEG, :]
        v_all[2 * me + half] = v_ref[half * SEG : (half + 1) * SEG, :]
    pl.semaphore_wait(barrier, 6)

    keys = Gather(k_all, gather_send.at[0], gather_recv.at[0])
    vals = Gather(v_all, gather_send.at[1], gather_recv.at[1])
    keys.own()

    for t in range(2):
        cur = parents[2 * me + t]
        for i in range(DEPTH):
            slots[t, i] = jnp.where(cur >= 0, cur, SEGS)
            cur = jnp.where(cur >= 0, parents[jnp.maximum(cur, 0)], -1)

    def find(j):
        for t in range(2):
            found = jnp.where(j == 2 * me + t, DEPTH, SLOTS)
            for i in range(DEPTH):
                found = jnp.where(slots[t, i] == j, i, found)
            where_to[t, j] = found

    loop(SEGS, find)

    locals_[0].wait()
    locals_[1].wait()

    def prepare(u):
        t = u // PAIRS
        first = lax.rem(u, PAIRS) * W
        rows = pl.ds(pl.multiple_of(t * SEG, SEG), SEG)
        for src, turned, stacked in ((q, qt, qs), (g, gt, gs)):
            for k in range(2):
                block = src[rows, pl.ds(pl.multiple_of(first + k * HD, HD), HD)]
                stacked[u, pl.ds(k * SEG, SEG), :] = block
                turned[u, :, pl.ds(k * SEG, SEG)] = block.T

    loop(UNITS, prepare)
    keys.forward()
    vals.own()
    vals.forward()

    for c in range(D // W):
        locals_[2 + c].wait()
        hid_t[pl.ds(c * W, W), :] = park(c)[...].T

    e, dp = (e0, e1), (dp0, dp1)
    keys.arrive()
    hidden = Hidden(hid_t, hid_got, hid_send, hid_recv)
    hidden.start()
    for t in range(2):
        head = k_all[2 * me + t, 0:16, :].astype(F32)[0:1]
        k_all[SEGS] = jnp.broadcast_to(head, (SEG, HD)).astype(BF)
        for i in range(SLOTS):
            block = k_all[slots[t, i]] if i < DEPTH else k_all[2 * me + t]
            kc[t, pl.ds(i * SEG, SEG), :] = block
            kct[t, :, pl.ds(i * SEG, SEG)] = block.T
    paired(
        lambda unit: score_steps(unit, kc, qt, e, mxs),
        lambda unit: prob_steps(unit, slots, e, mxs, inv, p),
    )

    def sums(i):
        buffers = (kv_stage, kv_own, kv_got, kv_mid, kv_last)
        return Reduce(
            *(b.at[i] for b in (*buffers, sum_send, sum_recv)), sum_send_on.at[i], sum_recv_on.at[i]
        )

    def project(i):
        buffers = (low, low_got, share_send, share_recv, pr_own, pr_mid, pr_last)
        return Project(
            hidden, *(b.at[i] for b in buffers), sum_send_on.at[2 + i], sum_recv_on.at[2 + i]
        )

    dv, dk, pv, pk = sums(0), sums(1), project(0), project(1)

    def side_block(rank, half):
        segment = 2 * rank + half
        return side[0, where_to[0, segment]] + side[1, where_to[1, segment]]

    for t in range(2):
        side_grad(t, p, gs, side)
    dv.scatter(side_block)

    vals.arrive()
    v_all[SEGS] = jnp.zeros((SEG, HD), BF)
    for t in range(2):
        for i in range(SLOTS):
            block = v_all[slots[t, i]] if i < DEPTH else v_all[2 * me + t]
            vc[t, pl.ds(i * SEG, SEG), :] = block
    paired(
        lambda unit: dprob_steps(unit, vc, gt, e, inv, dp, delta),
        lambda unit: dscore_steps(unit, e, inv, dp, delta, p),
    )
    for t in range(2):
        side_grad(t, p, qs, side)
    dk.scatter(side_block)
    loop(UNITS, lambda u: dq_unit(u, kct, p, dq_ref))
    dv.middle()
    dk.middle()
    pv.share(dv, 1.0)
    pk.share(dk, SCALE)
    pv.middle()
    pk.middle()
    for half in range(2):
        rows = pl.ds(half * (DCOLS // 2), DCOLS // 2)
        proj_ref[rows, pl.ds(HD, HD)] = pv.finish(half)
        proj_ref[rows, pl.ds(0, HD)] = pk.finish(half)
    for part in (keys, vals, hidden, dv, dk, pv, pk):
        part.drain()


def copy_kernel(dq_in, proj_in, dq_out, proj_out):
    dq_out[...] = dq_in[...]
    proj_out[...] = proj_in[...]


def on_device(hidden_in, queries, keys, values, out_grad, parents):
    vmem = pl.BlockSpec(memory_space=pltpu.VMEM)
    hbm = pl.BlockSpec(memory_space=pl.ANY)
    smem = pl.BlockSpec(memory_space=pltpu.SMEM)
    tokens = 2 * SEG
    half = DCOLS // 2
    scratch = [
        pltpu.VMEM((D, tokens), BF),
        pltpu.VMEM((tokens, GROUP * HD), BF),
        pltpu.VMEM((tokens, GROUP * HD), BF),
        pltpu.VMEM((SEGS + 1, SEG, HD), BF),
        pltpu.VMEM((SEGS + 1, SEG, HD), BF),
        pltpu.VMEM((2, KEYS, HD), BF),
        pltpu.VMEM((2, KEYS, HD), BF),
        pltpu.VMEM((2, HD, KEYS), BF),
        pltpu.VMEM((UNITS, HD, W), BF),
        pltpu.VMEM((UNITS, HD, W), BF),
        pltpu.VMEM((UNITS, W, HD), BF),
        pltpu.VMEM((UNITS, W, HD), BF),
        pltpu.VMEM((UNITS // 2, KEYS, W), F32),
        pltpu.VMEM((UNITS // 2, KEYS, W), F32),
        pltpu.VMEM((KEYS, W), F32),
        pltpu.VMEM((KEYS, W), F32),
        pltpu.VMEM((UNITS, KEYS, W), BF),
        pltpu.VMEM((UNITS, 8, W), F32),
        pltpu.VMEM((UNITS, 8, W), F32),
        pltpu.VMEM((UNITS, 8, W), F32),
        pltpu.VMEM((2, SLOTS + 1, SEG, HD), F32),
        pltpu.VMEM((2, tokens, HD), BF),
        pltpu.VMEM((2, 2, SIDE - 1, tokens, HD), BF),
        pltpu.VMEM((2, 2, SIDE - 1, SIDE, SEG, HD), BF),
        pltpu.VMEM((2, 2, SIDE, SEG, HD), F32),
        pltpu.VMEM((2, 2, SIDE - 1, SIDE, SEG, HD), BF),
        pltpu.VMEM((2, 2, SIDE - 1, SEG, HD), BF),
        pltpu.VMEM((2, 2, SIDE - 1, SEG, HD), BF),
        pltpu.VMEM((2, SIDE - 1, SIDE, half, tokens), BF),
        pltpu.VMEM((2, 2, SIDE, half, HD), F32),
        pltpu.VMEM((2, 2, SIDE - 1, half, HD), BF),
        pltpu.VMEM((2, 2, SIDE - 1, half, HD), BF),
        pltpu.SMEM((2, DEPTH), jnp.int32),
        pltpu.SMEM((2, SEGS), jnp.int32),
        pltpu.SemaphoreType.DMA((2 + D // W,)),
        pltpu.SemaphoreType.DMA((2, 2, RANKS)),
        pltpu.SemaphoreType.DMA((2, 2, RANKS)),
        pltpu.SemaphoreType.DMA((2, 2, SIDE, SIDE)),
        pltpu.SemaphoreType.DMA((2, 2, SIDE, SIDE)),
        pltpu.SemaphoreType.DMA((4, 2, SIDE)),
        pltpu.SemaphoreType.DMA((4, 2, SIDE)),
        pltpu.SemaphoreType.DMA((2, SIDE, SIDE)),
        pltpu.SemaphoreType.DMA((2, SIDE, SIDE)),
        pltpu.SemaphoreType.DMA((2, 2, SIDE)),
        pltpu.SemaphoreType.DMA((2, 2, SIDE)),
    ]
    out_shape = (
        jax.ShapeDtypeStruct((tokens, GROUP * HD), BF),
        jax.ShapeDtypeStruct((DCOLS, 2 * HD), F32),
    )
    grads = pl.pallas_call(
        kernel,
        out_shape=out_shape,
        in_specs=[hbm, hbm, vmem, vmem, hbm, smem],
        out_specs=(vmem, vmem),
        scratch_shapes=scratch,
        compiler_params=pltpu.CompilerParams(
            collective_id=1, has_side_effects=True, vmem_limit_bytes=62 << 20
        ),
    )(hidden_in, queries, keys, values, out_grad, parents)
    return pl.pallas_call(
        copy_kernel,
        out_shape=out_shape,
        in_specs=[vmem, vmem],
        out_specs=(vmem, vmem),
    )(*grads)


def solution(mesh):
    rows = P(("leaf", "seq"), None)
    return jax.shard_map(
        on_device,
        mesh=mesh,
        in_specs=(rows, rows, rows, rows, rows, P("leaf")),
        out_specs=(rows, rows),
        check_vma=False,
    )
```

```python
import functools

import jax
import jax.numpy as jnp
from jax import lax
from jax.experimental import pallas as pl
from jax.experimental.pallas import tpu as pltpu
from jax.sharding import PartitionSpec as P

BF, F32 = jnp.bfloat16, jnp.float32
MESH = pl.DeviceIdType.MESH
SIDE = 4
RANKS = SIDE * SIDE
SEG, HD, GROUP = 128, 128, 8
SEGS = 2 * RANKS
DEPTH = 16
SLOTS = DEPTH + 1
KEYS = SLOTS * SEG
PAIRS = GROUP // 2
UNITS = 2 * PAIRS
W = 2 * SEG
MC = 544
D = 5120
DCOLS = D // RANKS
LOG2E = 1.4426950408889634
SCALE = HD ** -0.5
PEN = 1e30
STEPS = (1, 3, 2)
NEAR, FAR = (1, 3), 2


def dot(a, b):
    return jnp.dot(a, b, preferred_element_type=F32)


def place():
    me = lax.axis_index("seq")
    return me, me // SIDE, lax.rem(me, SIDE)


def at(dy, dx):
    _, y, x = place()
    return lax.rem(y + dy + SIDE, SIDE) * SIDE + lax.rem(x + dx + SIDE, SIDE)


def remote(src, dst, send, recv, rank):
    return pltpu.make_async_remote_copy(
        src, dst, send, recv, device_id={"seq": rank}, device_id_type=MESH
    )


def loop(count, body):
    def step(index, carry):
        body(index)
        return carry

    lax.fori_loop(0, count, step, 0)


def interleave(*parts):
    timed = [((i + 0.5) / len(part), n, i) for n, part in enumerate(parts) for i in range(len(part))]
    for _, n, i in sorted(timed):
        parts[n][i]()


def paired(first, second):
    interleave(first((0, 0)))

    def body(i):
        interleave(first((1, i)), second((0, i)))
        interleave(first((0, i + 1)), second((1, i)))

    loop(UNITS // 2 - 1, body)
    end = UNITS // 2 - 1
    interleave(first((1, end)), second((0, end)))
    interleave(second((1, end)))


def score_steps(unit, kc, qt, e, mxs):
    parity, index = unit
    u, t = 2 * index + parity, index // 2
    weights = qt[u]
    state = [jnp.full((8, W), -3e38, F32)]

    def step(start):
        s = dot(kc[t, pl.ds(start, MC), :], weights)
        if start + MC == KEYS:
            key = lax.broadcasted_iota(jnp.int32, (SEG, W), 0)
            row = lax.broadcasted_iota(jnp.int32, (SEG, W), 1)
            row = jnp.where(row >= SEG, row - SEG, row)
            own = jnp.where(key <= row, s[MC - SEG :], -PEN)
            s = jnp.concatenate([s[: MC - SEG], own], axis=0)
        e[parity][index, pl.ds(start, MC), :] = s
        state[0] = jnp.maximum(state[0], jnp.max(s.reshape(MC // 8, 8, W), axis=0))
        if start + MC == KEYS:
            mxs[u] = state[0]

    return [functools.partial(step, start) for start in range(0, KEYS, MC)]


def prob_steps(unit, slots, e, mxs, inv, p):
    parity, index = unit
    u, t = 2 * index + parity, index // 2
    m = jnp.max(mxs[u], axis=0, keepdims=True) * (SCALE * LOG2E)
    state = [jnp.zeros((8, W), F32), None]

    def power(i):
        rows = pl.ds(i * SEG, SEG)
        shift = m
        if i < DEPTH:
            shift = m + jnp.where(slots[t, i] == SEGS, jnp.float32(PEN), jnp.float32(0.0))
        x = jnp.exp2(e[parity][index, rows, :] * (SCALE * LOG2E) - shift)
        e[parity][index, rows, :] = x
        state[0] += jnp.sum(x.reshape(SEG // 8, 8, W), axis=0)

    def norm(i):
        rows = pl.ds(i * SEG, SEG)
        if i == 0:
            state[1] = 1.0 / jnp.sum(state[0], axis=0, keepdims=True)
            inv[u] = jnp.broadcast_to(state[1], (8, W))
        p[u, rows, :] = (e[parity][index, rows, :] * state[1]).astype(BF)

    return [functools.partial(f, i) for f in (power, norm) for i in range(SLOTS)]


def dprob_steps(unit, vc, gt, e, inv, dp, delta):
    parity, index = unit
    u, t = 2 * index + parity, index // 2
    weights = gt[u]
    state = [jnp.zeros((8, W), F32)]

    def step(start):
        rows = pl.ds(start, MC)
        x = dot(vc[t, rows, :], weights)
        dp[parity][rows, :] = x
        x = x * e[parity][index, rows, :]
        state[0] += jnp.sum(x.reshape(MC // 8, 8, W), axis=0)
        if start + MC == KEYS:
            total = jnp.sum(state[0], axis=0, keepdims=True) * inv[u, 0:1, :]
            delta[u] = jnp.broadcast_to(total, (8, W))

    return [functools.partial(step, start) for start in range(0, KEYS, MC)]


def dscore_steps(unit, e, inv, dp, delta, ds):
    parity, index = unit
    u = 2 * index + parity
    r = inv[u, 0:1, :]
    d = delta[u, 0:1, :]

    def step(i):
        rows = pl.ds(i * SEG, SEG)
        ds[u, rows, :] = (e[parity][index, rows, :] * r * (dp[parity][rows, :] - d)).astype(BF)

    return [functools.partial(step, i) for i in range(SLOTS)]


def side_grad(t, lhs, rhs, acc):
    total = dot(lhs[t * PAIRS], rhs[t * PAIRS])
    for h in range(1, PAIRS):
        total += dot(lhs[t * PAIRS + h], rhs[t * PAIRS + h])
    acc[t, pl.ds(0, SLOTS)] = total.reshape(SLOTS, SEG, HD)
    acc[t, SLOTS] = jnp.zeros((SEG, HD), F32)


def dq_unit(u, kct, ds, dq):
    t = u // PAIRS
    g = (dot(kct[t], ds[u]) * SCALE).T.astype(BF)
    first = lax.rem(u, PAIRS) * W
    rows = pl.ds(pl.multiple_of(t * SEG, SEG), SEG)
    for k in range(2):
        dq[rows, pl.ds(pl.multiple_of(first + k * HD, HD), HD)] = g[k * SEG : (k + 1) * SEG]


class Gather:
    def __init__(self, buf, send, recv):
        self.buf, self.send, self.recv = buf, send, recv
        self.copies = {}

    def shift(self, half, first, second):
        return at(second, first) if half == 0 else at(first, second)

    def start(self, half, p, q, to_p, to_q):
        origin = 2 * self.shift(half, -p, -q) + half
        target = self.shift(half, to_p - p, to_q - q)
        sem = (half, to_p * SIDE + to_q)
        copy = remote(
            self.buf.at[origin], self.buf.at[origin], self.send.at[sem], self.recv.at[sem], target
        )
        copy.start()
        self.copies[half, to_p, to_q] = copy

    def own(self):
        for step in STEPS:
            for half in range(2):
                self.start(half, 0, 0, step, 0)
        for step in STEPS:
            for half in range(2):
                self.start(half, 0, 0, 0, step)

    def forward(self):
        for p in STEPS:
            for half in range(2):
                self.copies[half, p, 0].wait_recv()
                for q in STEPS:
                    self.start(half, p, 0, p, q)

    def arrive(self):
        for (half, p, q), copy in self.copies.items():
            if q:
                copy.wait_recv()

    def drain(self):
        for copy in self.copies.values():
            copy.wait_send()


class Reduce:
    def __init__(self, stage, own, got, mid, last, send, recv, send_on, recv_on):
        self.stage, self.own, self.got, self.mid, self.last = stage, own, got, mid, last
        self.send, self.recv, self.send_on, self.recv_on = send, recv, send_on, recv_on
        self.first, self.second = {}, {}

    def scatter(self, block):
        _, y, x = place()
        for step in (*STEPS, 0):
            for half in range(2):
                mine, other = ((x, y), (y, x))[half]
                column = lax.rem(mine + step, SIDE)
                for j in range(SIDE):
                    k = lax.rem(other + 1 + j, SIDE)
                    rank = k * SIDE + column if half == 0 else column * SIDE + k
                    value = block(rank, half)
                    if step == 0:
                        self.own[half, k] = value
                        continue
                    self.stage[half, step - 1, k] = value.astype(BF)
                    copy = remote(
                        self.stage.at[half, step - 1, k],
                        self.got.at[half, step - 1, k],
                        self.send.at[half, step, j],
                        self.recv.at[half, step, j],
                        (at(0, step), at(step, 0))[half],
                    )
                    copy.start()
                    self.first[half, step, j] = copy

    def total(self, half, j, k):
        for step in STEPS:
            self.first[half, step, j].wait_recv()
        total = self.own[half, k]
        for step in STEPS:
            total += self.got[half, step - 1, k].astype(F32)
        return total

    def middle(self):
        _, y, x = place()
        for j in range(SIDE):
            for half in range(2):
                k = lax.rem((y, x)[half] + 1 + j, SIDE)
                total = self.total(half, j, k)
                if j == SIDE - 1:
                    self.own[half, k] = total
                    continue
                self.mid[half, j] = total.astype(BF)
                copy = remote(
                    self.mid.at[half, j],
                    self.last.at[half, j],
                    self.send_on.at[half, j],
                    self.recv_on.at[half, j],
                    (at(j + 1, 0), at(0, j + 1))[half],
                )
                copy.start()
                self.second[half, j] = copy

    def finish(self, half):
        _, y, x = place()
        total = self.own[half, (y, x)[half]]
        for j in range(SIDE - 1):
            self.second[half, j].wait_recv()
            total += self.last[half, j].astype(F32)
        return total

    def drain(self):
        for copy in [*self.first.values(), *self.second.values()]:
            copy.wait_send()


class Hidden:
    def __init__(self, hid_t, got, send, recv):
        self.hid_t, self.got, self.send, self.recv = hid_t, got, send, recv
        self.copies, self.here = {}, set()

    def start(self, step):
        _, y, x = place()
        for half in range(2):
            column = lax.rem((x, y)[half] + step, SIDE)
            src = (self.hid_t.at[0, :, column], self.hid_t.at[1, column])[half]
            copy = remote(
                src,
                self.got.at[half, step // 2],
                self.send.at[half, step],
                self.recv.at[half, step],
                (at(0, step), at(step, 0))[half],
            )
            copy.start()
            self.copies[half, step] = copy

    def blocks(self, half, k):
        _, y, x = place()
        if half not in self.here:
            self.here.add(half)
            for step in NEAR:
                self.copies[half, step].wait_recv()
        own = self.hid_t[(0, k, x) if half == 0 else (1, y, k)]
        return [own, *(self.got[half, step // 2, k] for step in NEAR)]

    def drain(self):
        for copy in self.copies.values():
            copy.wait_send()


class Project(Reduce):
    def __init__(self, hidden, low, low_got, share_send, share_recv, stage, own, got, mid, last, *sems):
        super().__init__(stage, own, got, mid, last, None, None, *sems)
        self.hidden, self.low, self.low_got = hidden, low, low_got
        self.share_send, self.share_recv = share_send, share_recv

    def share(self, grad, scale):
        for half in range(2):
            self.low[pl.ds(half * SEG, SEG), :] = (grad.finish(half) * scale).astype(BF)
        for step in NEAR:
            for half in range(2):
                self.send_first(half, step, self.low, self.low_got.at[half, step // 2])
        _, y, x = place()
        for half in range(2):
            column = lax.rem((x, y)[half] + FAR, SIDE)
            for k in range(SIDE):
                block = self.hidden.hid_t[(0, k, column) if half == 0 else (1, column, k)]
                self.stage[half, k] = dot(block, self.low[...]).astype(BF)
            self.send_first(half, FAR, self.stage.at[half], self.got.at[half])

    def send_first(self, half, step, src, dst):
        sems = self.share_send.at[half, step], self.share_recv.at[half, step]
        copy = remote(src, dst, *sems, (at(0, step), at(step, 0))[half])
        copy.start()
        self.first[half, step] = copy

    def total(self, half, j, k):
        if j == 0:
            for step in STEPS:
                self.first[half, step].wait_recv()
        blocks = self.hidden.blocks(half, k)
        total = dot(blocks[0], self.low[...])
        for step, block in zip(NEAR, blocks[1:]):
            total += dot(block, self.low_got[half, step // 2])
        return total + self.got[half, k].astype(F32)


def kernel(
    hid_ref, q_ref, k_ref, v_ref, g_ref, parents,
    dq_ref, proj_ref,
    hid_t, q, g, k_all, v_all, kc, vc, kct, qt, gt, qs, gs,
    e0, e1, dp0, dp1, p, mxs, inv, delta, side, low, low_got,
    kv_stage, kv_own, kv_got, kv_mid, kv_last, hid_got, pr_stage, pr_own, pr_got, pr_mid, pr_last,
    slots, where_to, local_sem, gather_send, gather_recv,
    sum_send, sum_recv, sum_send_on, sum_recv_on,
    hid_send, hid_recv, share_send, share_recv,
):
    me, y, x = place()
    def park(c):
        return p.at[c % UNITS, pl.ds(c // UNITS * W, W), :]

    moves = [(q_ref, q), (g_ref, g)]
    moves += [(hid_ref.at[:, pl.ds(c * W, W)], park(c)) for c in range(D // W)]
    locals_ = [
        pltpu.make_async_copy(src, dst, local_sem.at[i]) for i, (src, dst) in enumerate(moves)
    ]
    for copy in locals_:
        copy.start()

    barrier = pltpu.get_barrier_semaphore()
    for step in STEPS:
        for mate in (at(0, step), at(step, 0)):
            pl.semaphore_signal(barrier, inc=1, device_id={"seq": mate}, device_id_type=MESH)
    for half in range(2):
        k_all[2 * me + half] = k_ref[half * SEG : (half + 1) * SEG, :]
        v_all[2 * me + half] = v_ref[half * SEG : (half + 1) * SEG, :]
    pl.semaphore_wait(barrier, 6)

    keys = Gather(k_all, gather_send.at[0], gather_recv.at[0])
    vals = Gather(v_all, gather_send.at[1], gather_recv.at[1])
    keys.own()

    for t in range(2):
        cur = parents[2 * me + t]
        for i in range(DEPTH):
            slots[t, i] = jnp.where(cur >= 0, cur, SEGS)
            cur = jnp.where(cur >= 0, parents[jnp.maximum(cur, 0)], -1)

    def find(j):
        for t in range(2):
            found = jnp.where(j == 2 * me + t, DEPTH, SLOTS)
            for i in range(DEPTH):
                found = jnp.where(slots[t, i] == j, i, found)
            where_to[t, j] = found

    loop(SEGS, find)

    locals_[0].wait()
    locals_[1].wait()

    def prepare(u):
        t = u // PAIRS
        first = lax.rem(u, PAIRS) * W
        rows = pl.ds(pl.multiple_of(t * SEG, SEG), SEG)
        for src, turned, stacked in ((q, qt, qs), (g, gt, gs)):
            for k in range(2):
                block = src[rows, pl.ds(pl.multiple_of(first + k * HD, HD), HD)]
                stacked[u, pl.ds(k * SEG, SEG), :] = block
                turned[u, :, pl.ds(k * SEG, SEG)] = block.T

    loop(UNITS, prepare)
    keys.forward()
    vals.own()
    for c in range(D // W):
        locals_[2 + c].wait()
        turned = park(c)[...].T
        first = c * W
        while first < (c + 1) * W:
            block, start = divmod(first, DCOLS // 2)
            size = min(DCOLS // 2 - start, (c + 1) * W - first)
            rank, half = divmod(block, 2)
            hid_t[half, rank // SIDE, rank % SIDE, pl.ds(start, size), :] = turned[
                first - c * W : first - c * W + size
            ]
            first += size

    e, dp = (e0, e1), (dp0, dp1)
    hidden = Hidden(hid_t, hid_got, hid_send, hid_recv)
    vals.forward()
    keys.arrive()
    hidden.start(1)
    hidden.start(3)
    for t in range(2):
        head = k_all[2 * me + t, 0:16, :].astype(F32)[0:1]
        k_all[SEGS] = jnp.broadcast_to(head, (SEG, HD)).astype(BF)
        for i in range(SLOTS):
            block = k_all[slots[t, i]] if i < DEPTH else k_all[2 * me + t]
            kc[t, pl.ds(i * SEG, SEG), :] = block
            kct[t, :, pl.ds(i * SEG, SEG)] = block.T
    paired(
        lambda unit: score_steps(unit, kc, qt, e, mxs),
        lambda unit: prob_steps(unit, slots, e, mxs, inv, p),
    )

    def sums(i):
        buffers = (kv_stage, kv_own, kv_got, kv_mid, kv_last)
        return Reduce(
            *(b.at[i] for b in (*buffers, sum_send, sum_recv)), sum_send_on.at[i], sum_recv_on.at[i]
        )

    def project(i):
        buffers = (low, low_got, share_send, share_recv, pr_stage, pr_own, pr_got, pr_mid, pr_last)
        return Project(
            hidden, *(b.at[i] for b in buffers), sum_send_on.at[2 + i], sum_recv_on.at[2 + i]
        )

    dv, dk, pv, pk = sums(0), sums(1), project(0), project(1)

    def side_block(rank, half):
        segment = 2 * rank + half
        return side[0, where_to[0, segment]] + side[1, where_to[1, segment]]

    for t in range(2):
        side_grad(t, p, gs, side)
    dv.scatter(side_block)

    vals.arrive()
    v_all[SEGS] = jnp.zeros((SEG, HD), BF)
    for t in range(2):
        for i in range(SLOTS):
            block = v_all[slots[t, i]] if i < DEPTH else v_all[2 * me + t]
            vc[t, pl.ds(i * SEG, SEG), :] = block
    paired(
        lambda unit: dprob_steps(unit, vc, gt, e, inv, dp, delta),
        lambda unit: dscore_steps(unit, e, inv, dp, delta, p),
    )
    for t in range(2):
        side_grad(t, p, qs, side)
    dk.scatter(side_block)
    loop(UNITS, lambda u: dq_unit(u, kct, p, dq_ref))
    dv.middle()
    dk.middle()
    pv.share(dv, 1.0)
    pk.share(dk, SCALE)
    pv.middle()
    pk.middle()
    for half in range(2):
        rows = pl.ds(half * (DCOLS // 2), DCOLS // 2)
        proj_ref[rows, pl.ds(HD, HD)] = pv.finish(half)
        proj_ref[rows, pl.ds(0, HD)] = pk.finish(half)
    for part in (keys, vals, hidden, dv, dk, pv, pk):
        part.drain()


def copy_kernel(dq_in, proj_in, dq_out, proj_out):
    dq_out[...] = dq_in[...]
    proj_out[...] = proj_in[...]


def on_device(hidden_in, queries, keys, values, out_grad, parents):
    vmem = pl.BlockSpec(memory_space=pltpu.VMEM)
    hbm = pl.BlockSpec(memory_space=pl.ANY)
    smem = pl.BlockSpec(memory_space=pltpu.SMEM)
    tokens = 2 * SEG
    half = DCOLS // 2
    scratch = [
        pltpu.VMEM((2, SIDE, SIDE, half, tokens), BF),
        pltpu.VMEM((tokens, GROUP * HD), BF),
        pltpu.VMEM((tokens, GROUP * HD), BF),
        pltpu.VMEM((SEGS + 1, SEG, HD), BF),
        pltpu.VMEM((SEGS + 1, SEG, HD), BF),
        pltpu.VMEM((2, KEYS, HD), BF),
        pltpu.VMEM((2, KEYS, HD), BF),
        pltpu.VMEM((2, HD, KEYS), BF),
        pltpu.VMEM((UNITS, HD, W), BF),
        pltpu.VMEM((UNITS, HD, W), BF),
        pltpu.VMEM((UNITS, W, HD), BF),
        pltpu.VMEM((UNITS, W, HD), BF),
        pltpu.VMEM((UNITS // 2, KEYS, W), F32),
        pltpu.VMEM((UNITS // 2, KEYS, W), F32),
        pltpu.VMEM((KEYS, W), F32),
        pltpu.VMEM((KEYS, W), F32),
        pltpu.VMEM((UNITS, KEYS, W), BF),
        pltpu.VMEM((UNITS, 8, W), F32),
        pltpu.VMEM((UNITS, 8, W), F32),
        pltpu.VMEM((UNITS, 8, W), F32),
        pltpu.VMEM((2, SLOTS + 1, SEG, HD), F32),
        pltpu.VMEM((2, tokens, HD), BF),
        pltpu.VMEM((2, 2, 2, tokens, HD), BF),
        pltpu.VMEM((2, 2, SIDE - 1, SIDE, SEG, HD), BF),
        pltpu.VMEM((2, 2, SIDE, SEG, HD), F32),
        pltpu.VMEM((2, 2, SIDE - 1, SIDE, SEG, HD), BF),
        pltpu.VMEM((2, 2, SIDE - 1, SEG, HD), BF),
        pltpu.VMEM((2, 2, SIDE - 1, SEG, HD), BF),
        pltpu.VMEM((2, 2, SIDE, half, tokens), BF),
        pltpu.VMEM((2, 2, SIDE, half, HD), BF),
        pltpu.VMEM((2, 2, SIDE, half, HD), F32),
        pltpu.VMEM((2, 2, SIDE, half, HD), BF),
        pltpu.VMEM((2, 2, SIDE - 1, half, HD), BF),
        pltpu.VMEM((2, 2, SIDE - 1, half, HD), BF),
        pltpu.SMEM((2, DEPTH), jnp.int32),
        pltpu.SMEM((2, SEGS), jnp.int32),
        pltpu.SemaphoreType.DMA((2 + D // W,)),
        pltpu.SemaphoreType.DMA((2, 2, RANKS)),
        pltpu.SemaphoreType.DMA((2, 2, RANKS)),
        pltpu.SemaphoreType.DMA((2, 2, SIDE, SIDE)),
        pltpu.SemaphoreType.DMA((2, 2, SIDE, SIDE)),
        pltpu.SemaphoreType.DMA((4, 2, SIDE)),
        pltpu.SemaphoreType.DMA((4, 2, SIDE)),
        pltpu.SemaphoreType.DMA((2, SIDE)),
        pltpu.SemaphoreType.DMA((2, SIDE)),
        pltpu.SemaphoreType.DMA((2, 2, SIDE)),
        pltpu.SemaphoreType.DMA((2, 2, SIDE)),
    ]
    out_shape = (
        jax.ShapeDtypeStruct((tokens, GROUP * HD), BF),
        jax.ShapeDtypeStruct((DCOLS, 2 * HD), F32),
    )
    grads = pl.pallas_call(
        kernel,
        out_shape=out_shape,
        in_specs=[hbm, hbm, vmem, vmem, hbm, smem],
        out_specs=(vmem, vmem),
        scratch_shapes=scratch,
        compiler_params=pltpu.CompilerParams(
            collective_id=1, has_side_effects=True, vmem_limit_bytes=62 << 20
        ),
    )(hidden_in, queries, keys, values, out_grad, parents)
    return pl.pallas_call(
        copy_kernel,
        out_shape=out_shape,
        in_specs=[vmem, vmem],
        out_specs=(vmem, vmem),
    )(*grads)


def solution(mesh):
    rows = P(("leaf", "seq"), None)
    return jax.shard_map(
        on_device,
        mesh=mesh,
        in_specs=(rows, rows, rows, rows, rows, P("leaf")),
        out_specs=(rows, rows),
        check_vma=False,
    )
```

```python
import functools

import jax
import jax.numpy as jnp
from jax import lax
from jax.experimental import pallas as pl
from jax.experimental.pallas import tpu as pltpu
from jax.sharding import PartitionSpec as P

BF, F32 = jnp.bfloat16, jnp.float32
MESH = pl.DeviceIdType.MESH
SIDE = 4
RANKS = SIDE * SIDE
SEG, HD, GROUP = 128, 128, 8
SEGS = 2 * RANKS
DEPTH = 16
SLOTS = DEPTH + 1
KEYS = SLOTS * SEG
PAIRS = GROUP // 2
UNITS = 2 * PAIRS
W = 2 * SEG
MC = 544
D = 5120
DCOLS = D // RANKS
LOG2E = 1.4426950408889634
SCALE = HD ** -0.5
PEN = 1e30
STEPS = (1, 3, 2)
NEAR, FAR = (1, 3), 2


def dot(a, b):
    return jnp.dot(a, b, preferred_element_type=F32)


def place():
    me = lax.axis_index("seq")
    return me, me // SIDE, lax.rem(me, SIDE)


def at(dy, dx):
    _, y, x = place()
    return lax.rem(y + dy + SIDE, SIDE) * SIDE + lax.rem(x + dx + SIDE, SIDE)


def remote(src, dst, send, recv, rank):
    return pltpu.make_async_remote_copy(
        src, dst, send, recv, device_id={"seq": rank}, device_id_type=MESH
    )


def loop(count, body):
    def step(index, carry):
        body(index)
        return carry

    lax.fori_loop(0, count, step, 0)


def interleave(*parts):
    timed = [((i + 0.5) / len(part), n, i) for n, part in enumerate(parts) for i in range(len(part))]
    for _, n, i in sorted(timed):
        parts[n][i]()


def paired(first, second):
    interleave(first((0, 0)))

    def body(i):
        interleave(first((1, i)), second((0, i)))
        interleave(first((0, i + 1)), second((1, i)))

    loop(UNITS // 2 - 1, body)
    end = UNITS // 2 - 1
    interleave(first((1, end)), second((0, end)))
    interleave(second((1, end)))


def score_steps(unit, kc, qt, e, mxs):
    parity, index = unit
    u, t = 2 * index + parity, index // 2
    weights = qt[u]
    state = [jnp.full((8, W), -3e38, F32)]

    def step(start):
        s = dot(kc[t, pl.ds(start, MC), :], weights)
        if start + MC == KEYS:
            key = lax.broadcasted_iota(jnp.int32, (SEG, W), 0)
            row = lax.broadcasted_iota(jnp.int32, (SEG, W), 1)
            row = jnp.where(row >= SEG, row - SEG, row)
            own = jnp.where(key <= row, s[MC - SEG :], -PEN)
            s = jnp.concatenate([s[: MC - SEG], own], axis=0)
        e[parity][index, pl.ds(start, MC), :] = s
        state[0] = jnp.maximum(state[0], jnp.max(s.reshape(MC // 8, 8, W), axis=0))
        if start + MC == KEYS:
            mxs[u] = state[0]

    return [functools.partial(step, start) for start in range(0, KEYS, MC)]


def prob_steps(unit, slots, e, mxs, inv, p):
    parity, index = unit
    u, t = 2 * index + parity, index // 2
    m = jnp.max(mxs[u], axis=0, keepdims=True) * (SCALE * LOG2E)
    state = [jnp.zeros((8, W), F32), None]

    def power(i):
        rows = pl.ds(i * SEG, SEG)
        shift = m
        if i < DEPTH:
            shift = m + jnp.where(slots[t, i] == SEGS, jnp.float32(PEN), jnp.float32(0.0))
        x = jnp.exp2(e[parity][index, rows, :] * (SCALE * LOG2E) - shift)
        e[parity][index, rows, :] = x
        state[0] += jnp.sum(x.reshape(SEG // 8, 8, W), axis=0)

    def norm(i):
        rows = pl.ds(i * SEG, SEG)
        if i == 0:
            state[1] = 1.0 / jnp.sum(state[0], axis=0, keepdims=True)
            inv[u] = jnp.broadcast_to(state[1], (8, W))
        p[u, rows, :] = (e[parity][index, rows, :] * state[1]).astype(BF)

    return [functools.partial(f, i) for f in (power, norm) for i in range(SLOTS)]


def dprob_steps(unit, vc, gt, e, inv, dp, delta):
    parity, index = unit
    u, t = 2 * index + parity, index // 2
    weights = gt[u]
    state = [jnp.zeros((8, W), F32)]

    def step(start):
        rows = pl.ds(start, MC)
        x = dot(vc[t, rows, :], weights)
        dp[parity][rows, :] = x
        x = x * e[parity][index, rows, :]
        state[0] += jnp.sum(x.reshape(MC // 8, 8, W), axis=0)
        if start + MC == KEYS:
            total = jnp.sum(state[0], axis=0, keepdims=True) * inv[u, 0:1, :]
            delta[u] = jnp.broadcast_to(total, (8, W))

    return [functools.partial(step, start) for start in range(0, KEYS, MC)]


def dscore_steps(unit, e, inv, dp, delta, ds):
    parity, index = unit
    u = 2 * index + parity
    r = inv[u, 0:1, :]
    d = delta[u, 0:1, :]

    def step(i):
        rows = pl.ds(i * SEG, SEG)
        ds[u, rows, :] = (e[parity][index, rows, :] * r * (dp[parity][rows, :] - d)).astype(BF)

    return [functools.partial(step, i) for i in range(SLOTS)]


def side_grad(t, lhs, rhs, acc):
    total = dot(lhs[t * PAIRS], rhs[t * PAIRS])
    for h in range(1, PAIRS):
        total += dot(lhs[t * PAIRS + h], rhs[t * PAIRS + h])
    acc[t, pl.ds(0, SLOTS)] = total.reshape(SLOTS, SEG, HD)
    acc[t, SLOTS] = jnp.zeros((SEG, HD), F32)


def dq_unit(u, kct, ds, dq):
    t = u // PAIRS
    g = (dot(kct[t], ds[u]) * SCALE).T.astype(BF)
    first = lax.rem(u, PAIRS) * W
    rows = pl.ds(pl.multiple_of(t * SEG, SEG), SEG)
    for k in range(2):
        dq[rows, pl.ds(pl.multiple_of(first + k * HD, HD), HD)] = g[k * SEG : (k + 1) * SEG]


class Gather:
    def __init__(self, buf, send, recv):
        self.buf, self.send, self.recv = buf, send, recv
        self.copies = {}

    def shift(self, half, first, second):
        return at(second, first) if half == 0 else at(first, second)

    def start(self, half, p, q, to_p, to_q):
        origin = 2 * self.shift(half, -p, -q) + half
        target = self.shift(half, to_p - p, to_q - q)
        sem = (half, to_p * SIDE + to_q)
        copy = remote(
            self.buf.at[origin], self.buf.at[origin], self.send.at[sem], self.recv.at[sem], target
        )
        copy.start()
        self.copies[half, to_p, to_q] = copy

    def own(self):
        for step in STEPS:
            for half in range(2):
                self.start(half, 0, 0, step, 0)
        for step in STEPS:
            for half in range(2):
                self.start(half, 0, 0, 0, step)

    def forward(self):
        for p in STEPS:
            for half in range(2):
                self.copies[half, p, 0].wait_recv()
                for q in STEPS:
                    self.start(half, p, 0, p, q)

    def arrive(self):
        for (half, p, q), copy in self.copies.items():
            if q:
                copy.wait_recv()

    def drain(self):
        for copy in self.copies.values():
            copy.wait_send()


class Reduce:
    def __init__(self, stage, own, got, mid, last, send, recv, send_on, recv_on):
        self.stage, self.own, self.got, self.mid, self.last = stage, own, got, mid, last
        self.send, self.recv, self.send_on, self.recv_on = send, recv, send_on, recv_on
        self.first, self.second = {}, {}

    def scatter(self, block):
        _, y, x = place()
        for j in range(SIDE):
            for step in (*STEPS, 0):
                for half in range(2):
                    mine, other = ((x, y), (y, x))[half]
                    column = lax.rem(mine + step, SIDE)
                    k = lax.rem(other + 1 + j, SIDE)
                    rank = k * SIDE + column if half == 0 else column * SIDE + k
                    value = block(rank, half)
                    if step == 0:
                        self.own[half, k] = value
                        continue
                    self.stage[half, step - 1, k] = value.astype(BF)
                    copy = remote(
                        self.stage.at[half, step - 1, k],
                        self.got.at[half, step - 1, k],
                        self.send.at[half, step, j],
                        self.recv.at[half, step, j],
                        (at(0, step), at(step, 0))[half],
                    )
                    copy.start()
                    self.first[half, step, j] = copy

    def total(self, half, j, k):
        for step in STEPS:
            self.first[half, step, j].wait_recv()
        total = self.own[half, k]
        for step in STEPS:
            total += self.got[half, step - 1, k].astype(F32)
        return total

    def middle(self):
        _, y, x = place()
        for j in range(SIDE):
            for half in range(2):
                k = lax.rem((y, x)[half] + 1 + j, SIDE)
                total = self.total(half, j, k)
                if j == SIDE - 1:
                    self.own[half, k] = total
                    continue
                self.mid[half, j] = total.astype(BF)
                copy = remote(
                    self.mid.at[half, j],
                    self.last.at[half, j],
                    self.send_on.at[half, j],
                    self.recv_on.at[half, j],
                    (at(j + 1, 0), at(0, j + 1))[half],
                )
                copy.start()
                self.second[half, j] = copy

    def finish(self, half):
        _, y, x = place()
        total = self.own[half, (y, x)[half]]
        for j in range(SIDE - 1):
            self.second[half, j].wait_recv()
            total += self.last[half, j].astype(F32)
        return total

    def drain(self):
        for copy in [*self.first.values(), *self.second.values()]:
            copy.wait_send()


class Hidden:
    def __init__(self, hid_t, got, send, recv):
        self.hid_t, self.got, self.send, self.recv = hid_t, got, send, recv
        self.copies, self.here = {}, set()

    def start(self, step):
        _, y, x = place()
        for half in range(2):
            column = lax.rem((x, y)[half] + step, SIDE)
            src = (self.hid_t.at[0, :, column], self.hid_t.at[1, column])[half]
            copy = remote(
                src,
                self.got.at[half, step // 2],
                self.send.at[half, step],
                self.recv.at[half, step],
                (at(0, step), at(step, 0))[half],
            )
            copy.start()
            self.copies[half, step] = copy

    def blocks(self, half, k):
        _, y, x = place()
        if half not in self.here:
            self.here.add(half)
            for step in NEAR:
                self.copies[half, step].wait_recv()
        own = self.hid_t[(0, k, x) if half == 0 else (1, y, k)]
        return [own, *(self.got[half, step // 2, k] for step in NEAR)]

    def drain(self):
        for copy in self.copies.values():
            copy.wait_send()


class Project(Reduce):
    def __init__(self, hidden, low, low_got, share_send, share_recv, stage, own, got, mid, last, *sems):
        super().__init__(stage, own, got, mid, last, None, None, *sems)
        self.hidden, self.low, self.low_got = hidden, low, low_got
        self.share_send, self.share_recv = share_send, share_recv

    def share(self, grad, scale):
        for half in range(2):
            self.low[pl.ds(half * SEG, SEG), :] = (grad.finish(half) * scale).astype(BF)
        for step in NEAR:
            for half in range(2):
                self.send_first(half, step, self.low, self.low_got.at[half, step // 2])
        _, y, x = place()
        for half in range(2):
            column = lax.rem((x, y)[half] + FAR, SIDE)
            for k in range(SIDE):
                block = self.hidden.hid_t[(0, k, column) if half == 0 else (1, column, k)]
                self.stage[half, k] = dot(block, self.low[...]).astype(BF)
            self.send_first(half, FAR, self.stage.at[half], self.got.at[half])

    def send_first(self, half, step, src, dst):
        sems = self.share_send.at[half, step], self.share_recv.at[half, step]
        copy = remote(src, dst, *sems, (at(0, step), at(step, 0))[half])
        copy.start()
        self.first[half, step] = copy

    def total(self, half, j, k):
        if j == 0:
            for step in STEPS:
                self.first[half, step].wait_recv()
        blocks = self.hidden.blocks(half, k)
        total = dot(blocks[0], self.low[...])
        for step, block in zip(NEAR, blocks[1:]):
            total += dot(block, self.low_got[half, step // 2])
        return total + self.got[half, k].astype(F32)


def kernel(
    hid_ref, q_ref, k_ref, v_ref, g_ref, parents,
    dq_ref, proj_ref,
    hid_t, q, g, k_all, v_all, kc, vc, kct, qt, gt, qs, gs,
    e0, e1, dp0, dp1, p, mxs, inv, delta, side, low, low_got,
    kv_stage, kv_own, kv_got, kv_mid, kv_last, hid_got, pr_stage, pr_own, pr_got, pr_mid, pr_last,
    slots, where_to, local_sem, gather_send, gather_recv,
    sum_send, sum_recv, sum_send_on, sum_recv_on,
    hid_send, hid_recv, share_send, share_recv,
):
    me, y, x = place()
    def park(c):
        return p.at[c % UNITS, pl.ds(c // UNITS * W, W), :]

    moves = [(q_ref, q), (g_ref, g)]
    moves += [(hid_ref.at[:, pl.ds(c * W, W)], park(c)) for c in range(D // W)]
    locals_ = [
        pltpu.make_async_copy(src, dst, local_sem.at[i]) for i, (src, dst) in enumerate(moves)
    ]
    for copy in locals_:
        copy.start()

    barrier = pltpu.get_barrier_semaphore()
    for step in STEPS:
        for mate in (at(0, step), at(step, 0)):
            pl.semaphore_signal(barrier, inc=1, device_id={"seq": mate}, device_id_type=MESH)
    for half in range(2):
        k_all[2 * me + half] = k_ref[half * SEG : (half + 1) * SEG, :]
        v_all[2 * me + half] = v_ref[half * SEG : (half + 1) * SEG, :]
    pl.semaphore_wait(barrier, 6)

    keys = Gather(k_all, gather_send.at[0], gather_recv.at[0])
    vals = Gather(v_all, gather_send.at[1], gather_recv.at[1])
    keys.own()

    for t in range(2):
        cur = parents[2 * me + t]
        for i in range(DEPTH):
            slots[t, i] = jnp.where(cur >= 0, cur, SEGS)
            cur = jnp.where(cur >= 0, parents[jnp.maximum(cur, 0)], -1)

    def find(j):
        for t in range(2):
            found = jnp.where(j == 2 * me + t, DEPTH, SLOTS)
            for i in range(DEPTH):
                found = jnp.where(slots[t, i] == j, i, found)
            where_to[t, j] = found

    loop(SEGS, find)

    locals_[0].wait()
    locals_[1].wait()

    def prepare(u):
        t = u // PAIRS
        first = lax.rem(u, PAIRS) * W
        rows = pl.ds(pl.multiple_of(t * SEG, SEG), SEG)
        for src, turned, stacked in ((q, qt, qs), (g, gt, gs)):
            for k in range(2):
                block = src[rows, pl.ds(pl.multiple_of(first + k * HD, HD), HD)]
                stacked[u, pl.ds(k * SEG, SEG), :] = block
                turned[u, :, pl.ds(k * SEG, SEG)] = block.T

    loop(UNITS, prepare)
    keys.forward()
    vals.own()
    for c in range(D // W):
        locals_[2 + c].wait()
        turned = park(c)[...].T
        first = c * W
        while first < (c + 1) * W:
            block, start = divmod(first, DCOLS // 2)
            size = min(DCOLS // 2 - start, (c + 1) * W - first)
            rank, half = divmod(block, 2)
            hid_t[half, rank // SIDE, rank % SIDE, pl.ds(start, size), :] = turned[
                first - c * W : first - c * W + size
            ]
            first += size

    e, dp = (e0, e1), (dp0, dp1)
    hidden = Hidden(hid_t, hid_got, hid_send, hid_recv)
    vals.forward()
    keys.arrive()
    hidden.start(1)
    hidden.start(3)
    for t in range(2):
        head = k_all[2 * me + t, 0:16, :].astype(F32)[0:1]
        k_all[SEGS] = jnp.broadcast_to(head, (SEG, HD)).astype(BF)
        for i in range(SLOTS):
            block = k_all[slots[t, i]] if i < DEPTH else k_all[2 * me + t]
            kc[t, pl.ds(i * SEG, SEG), :] = block
            kct[t, :, pl.ds(i * SEG, SEG)] = block.T
    paired(
        lambda unit: score_steps(unit, kc, qt, e, mxs),
        lambda unit: prob_steps(unit, slots, e, mxs, inv, p),
    )

    def sums(i):
        buffers = (kv_stage, kv_own, kv_got, kv_mid, kv_last)
        return Reduce(
            *(b.at[i] for b in (*buffers, sum_send, sum_recv)), sum_send_on.at[i], sum_recv_on.at[i]
        )

    def project(i):
        buffers = (low, low_got, share_send, share_recv, pr_stage, pr_own, pr_got, pr_mid, pr_last)
        return Project(
            hidden, *(b.at[i] for b in buffers), sum_send_on.at[2 + i], sum_recv_on.at[2 + i]
        )

    dv, dk, pv, pk = sums(0), sums(1), project(0), project(1)

    def side_block(rank, half):
        segment = 2 * rank + half
        return side[0, where_to[0, segment]] + side[1, where_to[1, segment]]

    for t in range(2):
        side_grad(t, p, gs, side)
    dv.scatter(side_block)

    vals.arrive()
    v_all[SEGS] = jnp.zeros((SEG, HD), BF)
    for t in range(2):
        for i in range(SLOTS):
            block = v_all[slots[t, i]] if i < DEPTH else v_all[2 * me + t]
            vc[t, pl.ds(i * SEG, SEG), :] = block
    paired(
        lambda unit: dprob_steps(unit, vc, gt, e, inv, dp, delta),
        lambda unit: dscore_steps(unit, e, inv, dp, delta, p),
    )
    for t in range(2):
        side_grad(t, p, qs, side)
    dk.scatter(side_block)
    loop(UNITS // 2, lambda u: dq_unit(u, kct, p, dq_ref))
    dv.middle()
    dk.middle()
    pv.share(dv, 1.0)
    loop(UNITS // 2, lambda u: dq_unit(u + UNITS // 2, kct, p, dq_ref))
    pk.share(dk, SCALE)
    pv.middle()
    pk.middle()
    for half in range(2):
        rows = pl.ds(half * (DCOLS // 2), DCOLS // 2)
        proj_ref[rows, pl.ds(HD, HD)] = pv.finish(half)
        proj_ref[rows, pl.ds(0, HD)] = pk.finish(half)
    for part in (keys, vals, hidden, dv, dk, pv, pk):
        part.drain()


def copy_kernel(dq_in, proj_in, dq_out, proj_out):
    dq_out[...] = dq_in[...]
    proj_out[...] = proj_in[...]


def on_device(hidden_in, queries, keys, values, out_grad, parents):
    vmem = pl.BlockSpec(memory_space=pltpu.VMEM)
    hbm = pl.BlockSpec(memory_space=pl.ANY)
    smem = pl.BlockSpec(memory_space=pltpu.SMEM)
    tokens = 2 * SEG
    half = DCOLS // 2
    scratch = [
        pltpu.VMEM((2, SIDE, SIDE, half, tokens), BF),
        pltpu.VMEM((tokens, GROUP * HD), BF),
        pltpu.VMEM((tokens, GROUP * HD), BF),
        pltpu.VMEM((SEGS + 1, SEG, HD), BF),
        pltpu.VMEM((SEGS + 1, SEG, HD), BF),
        pltpu.VMEM((2, KEYS, HD), BF),
        pltpu.VMEM((2, KEYS, HD), BF),
        pltpu.VMEM((2, HD, KEYS), BF),
        pltpu.VMEM((UNITS, HD, W), BF),
        pltpu.VMEM((UNITS, HD, W), BF),
        pltpu.VMEM((UNITS, W, HD), BF),
        pltpu.VMEM((UNITS, W, HD), BF),
        pltpu.VMEM((UNITS // 2, KEYS, W), F32),
        pltpu.VMEM((UNITS // 2, KEYS, W), F32),
        pltpu.VMEM((KEYS, W), F32),
        pltpu.VMEM((KEYS, W), F32),
        pltpu.VMEM((UNITS, KEYS, W), BF),
        pltpu.VMEM((UNITS, 8, W), F32),
        pltpu.VMEM((UNITS, 8, W), F32),
        pltpu.VMEM((UNITS, 8, W), F32),
        pltpu.VMEM((2, SLOTS + 1, SEG, HD), F32),
        pltpu.VMEM((2, tokens, HD), BF),
        pltpu.VMEM((2, 2, 2, tokens, HD), BF),
        pltpu.VMEM((2, 2, SIDE - 1, SIDE, SEG, HD), BF),
        pltpu.VMEM((2, 2, SIDE, SEG, HD), F32),
        pltpu.VMEM((2, 2, SIDE - 1, SIDE, SEG, HD), BF),
        pltpu.VMEM((2, 2, SIDE - 1, SEG, HD), BF),
        pltpu.VMEM((2, 2, SIDE - 1, SEG, HD), BF),
        pltpu.VMEM((2, 2, SIDE, half, tokens), BF),
        pltpu.VMEM((2, 2, SIDE, half, HD), BF),
        pltpu.VMEM((2, 2, SIDE, half, HD), F32),
        pltpu.VMEM((2, 2, SIDE, half, HD), BF),
        pltpu.VMEM((2, 2, SIDE - 1, half, HD), BF),
        pltpu.VMEM((2, 2, SIDE - 1, half, HD), BF),
        pltpu.SMEM((2, DEPTH), jnp.int32),
        pltpu.SMEM((2, SEGS), jnp.int32),
        pltpu.SemaphoreType.DMA((2 + D // W,)),
        pltpu.SemaphoreType.DMA((2, 2, RANKS)),
        pltpu.SemaphoreType.DMA((2, 2, RANKS)),
        pltpu.SemaphoreType.DMA((2, 2, SIDE, SIDE)),
        pltpu.SemaphoreType.DMA((2, 2, SIDE, SIDE)),
        pltpu.SemaphoreType.DMA((4, 2, SIDE)),
        pltpu.SemaphoreType.DMA((4, 2, SIDE)),
        pltpu.SemaphoreType.DMA((2, SIDE)),
        pltpu.SemaphoreType.DMA((2, SIDE)),
        pltpu.SemaphoreType.DMA((2, 2, SIDE)),
        pltpu.SemaphoreType.DMA((2, 2, SIDE)),
    ]
    out_shape = (
        jax.ShapeDtypeStruct((tokens, GROUP * HD), BF),
        jax.ShapeDtypeStruct((DCOLS, 2 * HD), F32),
    )
    grads = pl.pallas_call(
        kernel,
        out_shape=out_shape,
        in_specs=[hbm, hbm, vmem, vmem, hbm, smem],
        out_specs=(vmem, vmem),
        scratch_shapes=scratch,
        compiler_params=pltpu.CompilerParams(
            collective_id=1, has_side_effects=True, vmem_limit_bytes=62 << 20
        ),
    )(hidden_in, queries, keys, values, out_grad, parents)
    return pl.pallas_call(
        copy_kernel,
        out_shape=out_shape,
        in_specs=[vmem, vmem],
        out_specs=(vmem, vmem),
    )(*grads)


def solution(mesh):
    rows = P(("leaf", "seq"), None)
    return jax.shard_map(
        on_device,
        mesh=mesh,
        in_specs=(rows, rows, rows, rows, rows, P("leaf")),
        out_specs=(rows, rows),
        check_vma=False,
    )
```
